256 devices in a mesh: rep: 32 (over z, y), fsdp: 8 (over x, core).
Axes of the slice: x: 4, y: 4, z: 8, core: 2. Of those that a mesh axis runs over, the one named last changes fastest.
Arguments:
- gradient: bfloat16 [32, 2, 4096, 1024], P('rep', None, 'fsdp'), may hold values from -30 to 30
- feedback: float32 [32, 2, 4096, 1024], P('rep', None, 'fsdp'), may hold values from -3 to 3
- right_prior: float32 [2, 1024, 128], replicated, may hold values from -0.1875 to 0.1875
Outputs:
- new_feedback: float32 [32, 2, 4096, 1024], P('rep', None, 'fsdp')
- left_basis: float32 [2, 4096, 128], P(None, 'fsdp')
- right_factor: float32 [2, 1024, 128], replicated
The draws below stay inside these ranges and needn't reach their ends.
All inputs are finite; a program needn't handle non-finite values.
Results may differ from the reference program's by a relative error of at most 0.0003.
Values sent between devices are 32-bit elements; how exact they have to be, the bound alone decides.
No kernel may reach another device: no remote copies, remote signals or barrier semaphores. Data moves between devices by JAX's collectives and lax.ppermute only.
A program may use at most 64 MiB of HBM per device.

```python
import math
import jax
import jax.numpy as jnp
from jax import lax

FEATURES = 4096
KV_WIDTH = 1024
FACTOR_RANK = 128
MATRICES = 2
REPLICAS = 32


def draw_gradient(key, part):
    key = jax.random.fold_in(key, 11)
    keys = jax.random.split(key, 4)
    whole = (REPLICAS, MATRICES, FEATURES, KV_WIDTH)
    common = jax.random.truncated_normal(keys[0], -3.0, 3.0, whole[1:], jnp.float32)
    noise = jax.random.truncated_normal(keys[1], -3.0, 3.0, whole, jnp.float32)
    noise_weight = 0.7
    row_low = 0.3
    row_high = 3.0
    position = jnp.arange(FEATURES, dtype=jnp.float32) / FEATURES
    trend = jnp.power(3.0, position)
    row_scale = jnp.exp(jax.random.uniform(keys[2], (MATRICES, FEATURES), jnp.float32, math.log(row_low), math.log(row_high))) * trend[None, :]
    column_scale = jnp.exp(jax.random.uniform(keys[3], (MATRICES, KV_WIDTH), jnp.float32, math.log(0.3), math.log(3.0)))
    values = row_scale[None, :, :, None] * column_scale[None, :, None, :] * (common[None] + noise_weight * noise)
    return jnp.clip(values, -30.0, 30.0).astype(jnp.bfloat16)


def block_levels(own_key, shape, shards, least, high):
    def one(dim, shards_of):
        draws = jax.random.uniform(jax.random.fold_in(jax.random.fold_in(own_key, 6), dim), (shards_of,), jnp.float32, least / len(shards), high / len(shards))
        return jnp.repeat(jnp.exp(draws), shape[dim] // shards_of).reshape((-1,) + (1,) * (len(shape) - dim - 1))

    gain = one(*shards[0])
    for cut in shards[1:]:
        gain = gain * one(*cut)
    return gain


def centred(own_key, shape, spread, reach, cuts=(), kind=jnp.bfloat16):
    array = spread * jax.random.normal(own_key, shape, jnp.float32)
    if cuts:
        array = array * block_levels(own_key, shape, cuts, -0.22, 0.18)
    return jnp.clip(array, -reach, reach).astype(kind)


def setup_inputs(seed: int = 0) -> dict:
    arg_keys = jax.random.split(jax.random.key(seed), 4)
    return {
        "gradient": draw_gradient(jax.random.fold_in(arg_keys[3], 71), 0),
        "feedback": centred(arg_keys[1], (REPLICAS, MATRICES, FEATURES, KV_WIDTH), 0.5, 3.0, ((0, 32), (2, 8)), jnp.float32),
        "right_prior": centred(arg_keys[2], (MATRICES, KV_WIDTH, FACTOR_RANK), KV_WIDTH ** -0.5, 0.1875, (), jnp.float32),
    }


highest = lax.Precision.HIGHEST
ridge_relative = 0.001
ridge_absolute = 1e-06

def factorize(gram_mean):
    order = gram_mean.shape[1]
    trace_mean = jnp.trace(gram_mean, axis1=1, axis2=2) / order
    identity = jnp.eye(order, dtype=gram_mean.dtype)
    shifted = gram_mean + (ridge_relative * trace_mean + ridge_absolute)[:, None, None] * identity
    return jnp.linalg.cholesky(shifted)

def solve_rows(triangle, values):

    def single(factor, block):
        return jax.scipy.linalg.solve_triangular(factor, block.T, lower=True).T
    return jax.vmap(single)(triangle, values)

def reference(gradient, feedback, right_prior):
    replicas = gradient.shape[0]
    indices = jnp.arange(replicas, dtype=jnp.int32)

    def add_left(total, replica):
        merged = gradient[replica].astype(jnp.float32) + feedback[replica]
        return (total + jnp.einsum('mdk,mkr->mdr', merged, right_prior, precision=highest), None)
    start_left = jnp.zeros((MATRICES, FEATURES, FACTOR_RANK), jnp.float32)
    left_total = lax.scan(add_left, start_left, indices)[0]
    left_mean = left_total / replicas
    gram_mean = jnp.einsum('mdr,mds->mrs', left_mean, left_mean, precision=highest) / FEATURES
    triangle = factorize(gram_mean)
    left_basis = solve_rows(triangle, left_mean)

    def add_right(total, replica):
        merged = gradient[replica].astype(jnp.float32) + feedback[replica]
        return (total + jnp.einsum('mdk,mdr->mkr', merged, left_basis, precision=highest), None)
    start_right = jnp.zeros((MATRICES, KV_WIDTH, FACTOR_RANK), jnp.float32)
    right_total = lax.scan(add_right, start_right, indices)[0]
    norm_scale = 1.0 / math.sqrt(FEATURES)
    right_factor = right_total / replicas * norm_scale
    approx = jnp.einsum('mdr,mkr->mdk', left_basis, right_factor, precision=highest) * norm_scale

    def renew(replica):
        return gradient[replica].astype(jnp.float32) + feedback[replica] - approx
    new_feedback = lax.map(renew, indices)
    return (new_feedback, left_basis, right_factor)
```

```python
import math

import jax
import jax.numpy as jnp
from jax import lax
from jax.experimental import pallas as pl
from jax.experimental.pallas import tpu as pltpu
from jax.sharding import Mesh, PartitionSpec as P

FEATURES = 4096
WIDTH = 1024
RANK = 128
MATRICES = 2
ROWS = 512
ridge_relative = 0.001
ridge_absolute = 1e-06
MIB = 1 << 20
f32 = jnp.float32
bf16 = jnp.bfloat16


def halves(x):
    high = x.astype(bf16)
    return high, (x - high.astype(f32)).astype(bf16)


def dot(a, b, dims):
    return lax.dot_general(a, b, (dims, ((), ())), preferred_element_type=f32)


NN = ((1,), (0,))
NT = ((1,), (1,))
TN = ((0,), (0,))


def dot_wide(a, b):
    a_high, a_low = halves(a)
    b_high, b_low = halves(b)
    both = dot(a_high, jnp.concatenate([b_high, b_low], axis=1), NN)
    return both[:, :RANK] + (both[:, RANK:] + dot(a_low, b_high, NN))


def dot_deep(a, b):
    a_high, a_low = halves(a)
    b_high, b_low = halves(b)
    both = jnp.concatenate([a_high, a_low], axis=1)
    return dot(both, jnp.concatenate([b_high, b_high], axis=0), NN) + dot(a_high, b_low, NN)


def left_kernel(gradient, feedback, prior, left):
    merged = gradient[0].astype(f32) + feedback[0]
    left[:, 0] = dot_wide(merged, prior[0]).reshape(left.shape[0], 16, RANK)


def left_terms(gradient, feedback, right_prior):
    steps = 2
    rows = ROWS // steps
    return pl.pallas_call(
        left_kernel,
        grid=(MATRICES, steps),
        in_specs=[
            pl.BlockSpec((1, rows, WIDTH), lambda m, t: (m, t, 0)),
            pl.BlockSpec((1, rows, WIDTH), lambda m, t: (m, t, 0)),
            pl.BlockSpec((1, WIDTH, RANK), lambda m, t: (m, 0, 0)),
        ],
        out_specs=pl.BlockSpec((rows // 16, 1, 16, RANK), lambda m, t: (t, m, 0, 0)),
        out_shape=jax.ShapeDtypeStruct((ROWS // 16, MATRICES, 16, RANK), f32),
        compiler_params=pltpu.CompilerParams(vmem_limit_bytes=32 * MIB),
        name="left_terms",
    )(gradient, feedback, right_prior)


def right_kernel(gradient, feedback, left_mean, right, gram):
    left = left_mean[:, 0].reshape(ROWS, RANK)
    high, low = halves(left)
    both = jnp.concatenate([high, low], axis=1)

    @pl.when(pl.program_id(1) == 0)
    def _():
        square = dot(both, both, TN)
        gram[0] = square[:RANK, :RANK] + (square[RANK:, :RANK] + square[:RANK, RANK:] + square[RANK:, RANK:])

    merged_high, merged_low = halves(gradient[0].astype(f32) + feedback[0])
    double = dot(both, merged_high, TN)
    total = double[:RANK] + (double[RANK:] + dot(high, merged_low, TN))
    for j in range(right.shape[2]):
        right[0, :, j] = total[:, 128 * j : 128 * (j + 1)].reshape(16, 8, 128)


def right_terms(gradient, feedback, left_mean):
    steps = 2
    cols = WIDTH // steps
    return pl.pallas_call(
        right_kernel,
        grid=(MATRICES, steps),
        in_specs=[
            pl.BlockSpec((1, ROWS, cols), lambda m, t: (m, 0, t)),
            pl.BlockSpec((1, ROWS, cols), lambda m, t: (m, 0, t)),
            pl.BlockSpec((ROWS // 16, 1, 16, RANK), lambda m, t: (0, m, 0, 0)),
        ],
        out_specs=[
            pl.BlockSpec((1, 16, cols // 128, 8, 128), lambda m, t: (m, 0, t, 0, 0)),
            pl.BlockSpec((1, RANK, RANK), lambda m, t: (m, 0, 0)),
        ],
        out_shape=[
            jax.ShapeDtypeStruct((MATRICES, 16, WIDTH // 128, 8, 128), f32),
            jax.ShapeDtypeStruct((MATRICES, RANK, RANK), f32),
        ],
        compiler_params=pltpu.CompilerParams(vmem_limit_bytes=32 * MIB),
        name="right_terms",
    )(gradient, feedback, left_mean)


def inverse_kernel(parts, out):
    rows = lax.broadcasted_iota(jnp.int32, (RANK, RANK), 0)
    cols = lax.broadcasted_iota(jnp.int32, (RANK, RANK), 1)
    diagonal = rows == cols
    matrix = (parts[0] + parts[1] + (parts[2] + parts[3])) * (1.0 / FEATURES)
    trace = jnp.sum(jnp.where(diagonal, matrix, 0.0))
    ridge = ridge_relative * (trace / RANK) + ridge_absolute
    matrix = jnp.where(diagonal, matrix + ridge, matrix)
    unit = jnp.where(diagonal, 1.0, 0.0)
    for k in range(RANK - 1):
        low = k // 8 * 8
        row = matrix[k - low : k - low + 1]
        factor = matrix[:, k : k + 1] * (1.0 / row[:, k : k + 1])
        factor = jnp.where(rows[low:, :1] > k, factor, 0.0)
        unit_row = unit[k : k + 1]
        matrix = matrix - factor * row
        unit = jnp.concatenate([unit[:low], unit[low:] - factor * unit_row], axis=0) if low else unit - factor * unit_row
        if k % 8 == 7:
            out[low : low + 8] = matrix[:8]
            matrix = matrix[8:]
    out[RANK - 8 :] = matrix
    pivot = jnp.sum(jnp.where(diagonal, out[...], 0.0), axis=1, keepdims=True)
    out[...] = unit * lax.rsqrt(pivot)


def inverse_factor(parts):
    return pl.pallas_call(
        inverse_kernel,
        out_shape=jax.ShapeDtypeStruct((RANK, RANK), f32),
        compiler_params=pltpu.CompilerParams(vmem_limit_bytes=16 * MIB),
        name="inverse_factor",
    )(parts)


def finish_kernel(core, gradient, feedback, left_mean, inverse, right_total, renewed, basis, factor):
    norm_scale = 1.0 / math.sqrt(FEATURES)
    left = left_mean[:, 0].reshape(ROWS, RANK)
    left_basis = dot_wide(left, inverse[0].T)
    basis[0] = left_basis
    total = jnp.concatenate([right_total[0, :, j].reshape(RANK, 128) for j in range(WIDTH // 128)], axis=1)
    right = dot_deep(inverse[0], total) * (norm_scale / 32)
    factor[0] = right.T
    approx = dot_deep(left_basis * norm_scale, right)
    renewed[0] = gradient[0].astype(f32) + feedback[0] - approx


def finish(core, gradient, feedback, left_mean, inverse, right_total):
    mine = lambda i, core: i ^ core[0]
    return pl.pallas_call(
        finish_kernel,
        grid_spec=pltpu.PrefetchScalarGridSpec(
            num_scalar_prefetch=1,
            grid=(MATRICES,),
            in_specs=[
                pl.BlockSpec((1, ROWS, WIDTH), lambda i, core: (i ^ core[0], 0, 0)),
                pl.BlockSpec((1, ROWS, WIDTH), lambda i, core: (i ^ core[0], 0, 0)),
                pl.BlockSpec((ROWS // 16, 1, 16, RANK), lambda i, core: (0, i ^ core[0], 0, 0)),
                pl.BlockSpec((1, RANK, RANK), lambda i, core: (i, 0, 0)),
                pl.BlockSpec((1, 16, WIDTH // 128, 8, 128), lambda i, core: (i, 0, 0, 0, 0)),
            ],
            out_specs=[
                pl.BlockSpec((1, ROWS, WIDTH), lambda i, core: (i ^ core[0], 0, 0)),
                pl.BlockSpec((1, ROWS, RANK), lambda i, core: (i ^ core[0], 0, 0)),
                pl.BlockSpec((1, WIDTH, RANK), lambda i, core: (i ^ core[0], 0, 0)),
            ],
        ),
        out_shape=[
            jax.ShapeDtypeStruct((MATRICES, ROWS, WIDTH), f32),
            jax.ShapeDtypeStruct((MATRICES, ROWS, RANK), f32),
            jax.ShapeDtypeStruct((MATRICES, WIDTH, RANK), f32),
        ],
        compiler_params=pltpu.CompilerParams(vmem_limit_bytes=40 * MIB),
        name="finish",
    )(core, gradient, feedback, left_mean, inverse, right_total)


def spread(x, axes, size):
    return lax.all_to_all(jnp.broadcast_to(x[None], (size,) + x.shape), axes, 0, 0, tiled=True)


def swap(x):
    return lax.ppermute(x, "core", [(0, 1), (1, 0)])


def shards(gradient, feedback, right_prior):
    gradient, feedback = gradient[0], feedback[0]
    core = lax.axis_index("core")
    rep = ("z", "y")
    chips = ("z", "y", "x")
    left = left_terms(gradient, feedback, right_prior)
    left = lax.all_to_all(left, rep, 0, 0, tiled=True).sum(0) * (1.0 / 32)
    left_mean = spread(left, rep, 32)
    right, gram = right_terms(gradient, feedback, left_mean)
    pick = lambda x, i: lax.dynamic_index_in_dim(x, i, 0, False)
    gram = pick(gram, core) + swap(pick(gram, 1 - core))
    own = pick(right, core) + swap(pick(right, 1 - core))
    own = lax.all_to_all(own.reshape(128, 8, 128), chips, 0, 0, tiled=True).sum(0)
    inverse = inverse_factor(spread(gram, "x", 4))
    inverse = jnp.stack([inverse, swap(inverse)])
    own = spread(own, chips, 128).reshape(16, 8, 8, 128)
    total = jnp.stack([own, swap(own)])
    renewed, basis, factor = finish(core[None], gradient, feedback, left_mean, inverse, total)
    return renewed[None], basis, factor


def solution(mesh):
    chips = Mesh(mesh.devices.reshape(8, 4, 4, 2), ("z", "y", "x", "core"))
    rep, fsdp = ("z", "y"), ("x", "core")
    in_specs = (P(rep, None, fsdp, None), P(rep, None, fsdp, None), P())
    out_specs = (P(rep, None, fsdp, None), P(None, fsdp, None), P())
    return jax.shard_map(shards, mesh=chips, in_specs=in_specs, out_specs=out_specs, check_vma=False)
```

```python
import functools
import math

import jax
import jax.numpy as jnp
from jax import lax
from jax.experimental import pallas as pl
from jax.experimental.pallas import tpu as pltpu
from jax.sharding import Mesh, PartitionSpec as P

FEATURES = 4096
WIDTH = 1024
RANK = 128
MATRICES = 2
ROWS = 512
ridge_relative = 0.001
ridge_absolute = 1e-06
MIB = 1 << 20
f32 = jnp.float32
bf16 = jnp.bfloat16


def halves(x):
    high = x.astype(bf16)
    return high, (x - high.astype(f32)).astype(bf16)


def dot(a, b, dims):
    return lax.dot_general(a, b, (dims, ((), ())), preferred_element_type=f32)


def in_vmem(x):
    return pltpu.with_memory_space_constraint(x, pltpu.VMEM)


def in_hbm(x):
    return pltpu.with_memory_space_constraint(x, pltpu.HBM)


NN = ((1,), (0,))
NT = ((1,), (1,))
TN = ((0,), (0,))


def dot_wide(a, b):
    a_high, a_low = halves(a)
    b_high, b_low = halves(b)
    both = dot(a_high, jnp.concatenate([b_high, b_low], axis=1), NN)
    return both[:, :RANK] + (both[:, RANK:] + dot(a_low, b_high, NN))


def dot_deep(a, b):
    a_high, a_low = halves(a)
    b_high, b_low = halves(b)
    both = jnp.concatenate([a_high, a_low], axis=1)
    return dot(both, jnp.concatenate([b_high, b_high], axis=1), NT) + dot(a_high, b_low, NT)


def left_kernel(which, gradient, feedback, prior, left, merged, gradient_in, feedback_in, prior_in, sems, prior_sem):
    del which
    steps = gradient_in.shape[0]
    rows = ROWS * MATRICES // steps
    per = steps // MATRICES

    def fetch(i):
        m, at = i // per, i % per * rows
        return (
            pltpu.make_async_copy(gradient.at[m, pl.ds(at, rows)], gradient_in.at[i], sems.at[0, i]),
            pltpu.make_async_copy(feedback.at[m, pl.ds(at, rows)], feedback_in.at[i], sems.at[1, i]),
        )

    def fetch_prior(m):
        return pltpu.make_async_copy(prior.at[m], prior_in.at[m], prior_sem.at[m])

    for i in range(steps):
        if i % per == 0:
            fetch_prior(i // per).start()
        for copy in fetch(i):
            copy.start()
    for i in range(steps):
        m, at = i // per, i % per * rows
        if at == 0:
            fetch_prior(m).wait()
        for copy in fetch(i):
            copy.wait()
        total = gradient_in[i].astype(f32) + feedback_in[i]
        merged[m, at : at + rows] = total
        left[at // 16 : (at + rows) // 16, m] = dot_wide(total, prior_in[m]).reshape(rows // 16, 16, RANK)


def left_terms(which, gradient, feedback, right_prior, steps=4):
    rows = ROWS * MATRICES // steps
    return pl.pallas_call(
        left_kernel,
        in_specs=[pl.BlockSpec(memory_space=pltpu.SMEM)] + [pl.BlockSpec(memory_space=pltpu.HBM)] * 3,
        out_specs=[pl.BlockSpec(memory_space=pltpu.VMEM)] * 2,
        out_shape=[
            jax.ShapeDtypeStruct((ROWS // 16, MATRICES, 16, RANK), f32),
            jax.ShapeDtypeStruct((MATRICES, ROWS, WIDTH), f32),
        ],
        scratch_shapes=[
            pltpu.VMEM((steps, rows, WIDTH), bf16),
            pltpu.VMEM((steps, rows, WIDTH), f32),
            pltpu.VMEM((MATRICES, WIDTH, RANK), f32),
            pltpu.SemaphoreType.DMA((2, steps)),
            pltpu.SemaphoreType.DMA((MATRICES,)),
        ],
        compiler_params=pltpu.CompilerParams(vmem_limit_bytes=24 * MIB),
        name="left_terms",
    )(which, gradient, feedback, right_prior)


def stacked(left):
    return jnp.concatenate(halves(left), axis=1)


def gram_of(both):
    square = dot(both, both, TN)
    return square[:RANK, :RANK] + (square[RANK:, :RANK] + square[:RANK, RANK:] + square[RANK:, RANK:])


def right_kernel(which, merged, left_mean, right, *grams):
    i = which[0]
    both = stacked(left_mean[:, i].reshape(ROWS, RANK))
    if grams:
        grams[0][...] = gram_of(both)
        grams[1][...] = gram_of(stacked(left_mean[:, 1 - i].reshape(ROWS, RANK)))
    cols = WIDTH // 2
    for at in range(0, WIDTH, cols):
        merged_high, merged_low = halves(merged[i, :, at : at + cols])
        double = dot(both, merged_high, TN)
        total = double[:RANK] + (double[RANK:] + dot(both[:, :RANK], merged_low, TN))
        right[at : at + cols] = total.T


def right_terms(which, merged, left_mean, with_gram):
    square = jax.ShapeDtypeStruct((RANK, RANK), f32)
    return pl.pallas_call(
        right_kernel,
        in_specs=[pl.BlockSpec(memory_space=pltpu.SMEM)] + [pl.BlockSpec(memory_space=pltpu.VMEM)] * 2,
        out_shape=[jax.ShapeDtypeStruct((WIDTH, RANK), f32)] + [square] * (2 * with_gram),
        compiler_params=pltpu.CompilerParams(vmem_limit_bytes=24 * MIB),
        cost_estimate=pl.CostEstimate(flops=8 * 10**8, bytes_accessed=4 * 10**6, transcendentals=0),
        name="right_terms",
    )(which, merged, left_mean)


def tree_sum(terms):
    while len(terms) > 1:
        terms = [a + b for a, b in zip(terms[::2], terms[1::2])]
    return terms[0]


def inverse_kernel(gram, one, two, three, out):
    rows = lax.broadcasted_iota(jnp.int32, (RANK, RANK), 0)
    cols = lax.broadcasted_iota(jnp.int32, (RANK, RANK), 1)
    diagonal = rows == cols
    matrix = (gram[...] + one[...] + (two[...] + three[...])) * (1.0 / FEATURES)
    trace = jnp.sum(jnp.where(diagonal, matrix, 0.0))
    ridge = ridge_relative * (trace / RANK) + ridge_absolute
    matrix = jnp.where(diagonal, matrix + ridge, matrix)
    unit = jnp.where(diagonal, 1.0, 0.0)
    panels = RANK // 8
    left = [matrix[8 * q : 8 * q + 8] for q in range(panels)]
    right = [unit[8 * q : 8 * q + 8] for q in range(panels)]
    row = lax.broadcasted_iota(jnp.int32, (8, RANK), 0)

    def wide(x):
        return jnp.broadcast_to(x, (8, RANK))

    for p in range(panels):
        at = 8 * p
        col = [wide(left[p][:, at + j : at + j + 1]) for j in range(8)]
        solved_left, solved_right, reduced = left[p], right[p], right[p]
        pivots = scales = jnp.ones((8, RANK), f32)
        for j in range(8):
            pivot = wide(col[j][j : j + 1])
            scale = 1.0 / pivot
            factor = col[j] * scale
            below = jnp.where(row > j, factor, 0.0)
            beside = jnp.where(row != j, factor, 0.0)
            pivots = jnp.where(row == j, pivot, pivots)
            scales = jnp.where(row == j, scale, scales)
            row_left, row_right = wide(solved_left[j : j + 1]), wide(reduced[j : j + 1])
            for t in range(j + 1, 8):
                col[t] = col[t] - beside * wide(col[t][j : j + 1])
            solved_left = solved_left - beside * row_left
            solved_right = solved_right - beside * row_right
            reduced = reduced - below * row_right
        out[at : at + 8] = reduced * lax.rsqrt(pivots)
        solved_left, solved_right = solved_left * scales, solved_right * scales
        row_left = [wide(solved_left[j : j + 1]) for j in range(8)]
        row_right = [wide(solved_right[j : j + 1]) for j in range(8)]
        for q in range(p + 1, panels):
            col = [wide(left[q][:, at + j : at + j + 1]) for j in range(8)]
            left[q] = left[q] - tree_sum([c * r for c, r in zip(col, row_left)])
            right[q] = right[q] - tree_sum([c * r for c, r in zip(col, row_right)])


def inverse_factor(*grams):
    return pl.pallas_call(
        inverse_kernel,
        out_shape=jax.ShapeDtypeStruct((RANK, RANK), f32),
        compiler_params=pltpu.CompilerParams(vmem_limit_bytes=16 * MIB),
        cost_estimate=pl.CostEstimate(flops=3 * 10**9, bytes_accessed=10**5, transcendentals=0),
        name="inverse_factor",
    )(*grams)


def basis_kernel(core, left_mean, own, other, basis, operand, token):
    token[...] = jnp.zeros(token.shape, f32)
    for i, inverse in ((core[0], own), (1 - core[0], other)):
        rows = dot_wide(left_mean[:, i].reshape(ROWS, RANK), inverse[...].T)
        basis[i] = rows
        operand[i] = stacked(rows * (1.0 / math.sqrt(FEATURES)))


def basis_rows(core, left_mean, own, other):
    return pl.pallas_call(
        basis_kernel,
        in_specs=[pl.BlockSpec(memory_space=pltpu.SMEM)] + [pl.BlockSpec(memory_space=pltpu.VMEM)] * 3,
        out_shape=[
            jax.ShapeDtypeStruct((MATRICES, ROWS, RANK), f32),
            jax.ShapeDtypeStruct((MATRICES, ROWS, 2 * RANK), bf16),
            jax.ShapeDtypeStruct((8, RANK), f32),
        ],
        compiler_params=pltpu.CompilerParams(vmem_limit_bytes=16 * MIB),
        cost_estimate=pl.CostEstimate(flops=8 * 10**8, bytes_accessed=2 * 10**6, transcendentals=0),
        name="basis_rows",
    )(core, left_mean, own, other)


def factor_kernel(parts, inverse, out):
    total = tree_sum([parts[i] for i in range(parts.shape[0])])
    rows = dot_wide(total, inverse[...].T) * (1.0 / (32 * math.sqrt(FEATURES)))
    for i in range(out.shape[0]):
        out[i] = rows


def factor_rows(parts, inverse, copies):
    return pl.pallas_call(
        factor_kernel,
        out_shape=jax.ShapeDtypeStruct((copies,) + parts.shape[1:], f32),
        compiler_params=pltpu.CompilerParams(vmem_limit_bytes=16 * MIB),
        cost_estimate=pl.CostEstimate(flops=10**8, bytes_accessed=4 * 10**5, transcendentals=0),
        name="factor_rows",
    )(parts, inverse)


def tie_kernel(x, after, out):
    del x, after, out


def tie(x, after):
    return pl.pallas_call(
        tie_kernel,
        in_specs=[pl.BlockSpec(memory_space=pl.ANY), pl.BlockSpec(memory_space=pltpu.VMEM)],
        out_specs=pl.BlockSpec(memory_space=pl.ANY),
        out_shape=pltpu.VMEM(x.shape, x.dtype),
        input_output_aliases={0: 0},
        compiler_params=pltpu.CompilerParams(vmem_limit_bytes=MIB),
        name="tie",
    )(in_vmem(x), after)


def finish_kernel(which, gradient, feedback, operand, right, *rest):
    renewed, factor, gradient_in, feedback_in, renewed_out, turned, sems = rest[-7:]
    w = which[0]
    steps = gradient_in.shape[0]
    rows = ROWS // steps

    def fetch(i):
        at = pl.ds(i * rows, rows)
        return (
            pltpu.make_async_copy(gradient.at[w, at], gradient_in.at[i], sems.at[0, i]),
            pltpu.make_async_copy(feedback.at[w, at], feedback_in.at[i], sems.at[1, i]),
        )

    def store(i):
        return pltpu.make_async_copy(renewed_out.at[i], renewed.at[w, pl.ds(i * rows, rows)], sems.at[2, i])

    for i in range(steps):
        for copy in fetch(i):
            copy.start()
    store_factor = pltpu.make_async_copy(right, factor.at[w], sems.at[2, steps])
    store_factor.start()
    high, low = halves(right[...])
    turned[:, :RANK] = high
    turned[:, RANK : 2 * RANK] = high
    turned[:, 2 * RANK :] = low
    for i in range(steps):
        both = operand[w, i * rows : (i + 1) * rows]
        approx = dot(both, turned[:, : 2 * RANK], NT) + dot(both[:, :RANK], turned[:, 2 * RANK :], NT)
        for copy in fetch(i):
            copy.wait()
        renewed_out[i] = gradient_in[i].astype(f32) + feedback_in[i] - approx
        store(i).start()
    store_factor.wait()
    for i in range(steps):
        store(i).wait()


def finish(which, gradient, feedback, operand, right, before=(), steps=2):
    rows = ROWS // steps
    return pl.pallas_call(
        finish_kernel,
        in_specs=[pl.BlockSpec(memory_space=pltpu.SMEM)]
        + [pl.BlockSpec(memory_space=pltpu.HBM)] * 2
        + [pl.BlockSpec(memory_space=pltpu.VMEM)] * 2
        + [pl.BlockSpec(memory_space=pl.ANY)] * len(before),
        out_specs=[pl.BlockSpec(memory_space=pl.ANY)] * 2,
        out_shape=[
            jax.ShapeDtypeStruct((MATRICES, ROWS, WIDTH), f32),
            jax.ShapeDtypeStruct((MATRICES, WIDTH, RANK), f32),
        ],
        scratch_shapes=[
            pltpu.VMEM((steps, rows, WIDTH), bf16),
            pltpu.VMEM((steps, rows, WIDTH), f32),
            pltpu.VMEM((steps, rows, WIDTH), f32),
            pltpu.VMEM((WIDTH, 3 * RANK), bf16),
            pltpu.SemaphoreType.DMA((3, steps + 1)),
        ],
        input_output_aliases={5: 0, 6: 1} if before else {},
        compiler_params=pltpu.CompilerParams(vmem_limit_bytes=24 * MIB),
        cost_estimate=pl.CostEstimate(flops=8 * 10**8, bytes_accessed=6 * 10**6, transcendentals=0),
        name="finish",
    )(which, gradient, feedback, operand, right, *before)


def share_kernel(parts, *rest, scale):
    total = tree_sum([parts[i] for i in range(parts.shape[0])]) * scale
    out = rest[-1]
    for i in range(out.shape[0]):
        out[i] = total


def share(parts, copies, scale, after=()):
    return pl.pallas_call(
        functools.partial(share_kernel, scale=scale),
        out_shape=jax.ShapeDtypeStruct((copies,) + parts.shape[1:], f32),
        compiler_params=pltpu.CompilerParams(vmem_limit_bytes=8 * MIB),
        name="share",
    )(parts, *after)


def add_kernel(*refs):
    pairs = len(refs) // 3
    for i in range(pairs):
        refs[2 * pairs + i][...] = refs[2 * i][...] + refs[2 * i + 1][...]


def add_pairs(*arrays):
    return pl.pallas_call(
        add_kernel,
        out_shape=[jax.ShapeDtypeStruct(x.shape, f32) for x in arrays[::2]],
        compiler_params=pltpu.CompilerParams(vmem_limit_bytes=8 * MIB),
        name="add_pairs",
    )(*arrays)


def exchange(x, axes):
    return lax.all_to_all(x, axes, 0, 0, tiled=True)


def swap(x):
    return lax.ppermute(x, "core", [(0, 1), (1, 0)])


def shards(gradient, feedback, right_prior):
    own = lax.axis_index("core")[None]
    other = 1 - own
    rep, plane = ("z", "y"), ("y", "x")
    gradient, feedback, right_prior = in_hbm(gradient[0]), in_hbm(feedback[0]), in_hbm(right_prior)
    left, merged = left_terms(other, gradient, feedback, right_prior)
    left_mean = exchange(share(exchange(left, rep), 32, 1.0 / 32), rep)

    right_other, gram_other, gram = right_terms(other, merged, left_mean, True)
    right_other, gram_other = swap(right_other), swap(gram_other)
    right = right_terms(own, merged, left_mean, False)[0]
    total, gram = add_pairs(right, right_other, gram, gram_other)

    total = exchange(total.reshape(16, WIDTH // 16, RANK), plane)
    grams = [lax.ppermute(gram, "x", [(i, (i + s) % 4) for i in range(4)]) for s in (1, 3, 2)]
    total = exchange(share(total, 8, 1.0, grams), "z")
    inverse = inverse_factor(gram, *grams)
    right = exchange(factor_rows(total, inverse, 16), plane).reshape(WIDTH, RANK)
    basis, operand, token = basis_rows(own, left_mean, inverse, swap(inverse))
    right = tie(right, token)

    done = finish(own, gradient, feedback, operand, right)
    renewed, factor = finish(other, gradient, feedback, operand, swap(right), tuple(done))
    return renewed[None], basis, factor


def solution(mesh):
    chips = Mesh(mesh.devices.reshape(8, 4, 4, 2), ("z", "y", "x", "core"))
    rep, fsdp = ("z", "y"), ("x", "core")
    in_specs = (P(rep, None, fsdp, None), P(rep, None, fsdp, None), P())
    out_specs = (P(rep, None, fsdp, None), P(None, fsdp, None), P())
    return jax.shard_map(shards, mesh=chips, in_specs=in_specs, out_specs=out_specs, check_vma=False)
```

```python
import functools
import math

import jax
import jax.numpy as jnp
from jax import lax
from jax.experimental import pallas as pl
from jax.experimental.pallas import tpu as pltpu
from jax.sharding import Mesh, PartitionSpec as P

FEATURES = 4096
WIDTH = 1024
RANK = 128
MATRICES = 2
ROWS = 512
CHUNK = 64
BOX = 32
SHARE = WIDTH // BOX
PIECE = 16
ridge_relative = 0.001
ridge_absolute = 1e-06
MIB = 1 << 20
f32 = jnp.float32
bf16 = jnp.bfloat16


def halves(x):
    high = x.astype(bf16)
    return high, (x - high.astype(f32)).astype(bf16)


def dot(a, b, dims):
    return lax.dot_general(a, b, (dims, ((), ())), preferred_element_type=f32)


def in_vmem(x):
    return pltpu.with_memory_space_constraint(x, pltpu.VMEM)


def in_hbm(x):
    return pltpu.with_memory_space_constraint(x, pltpu.HBM)


NN = ((1,), (0,))
NT = ((1,), (1,))
TN = ((0,), (0,))


def dot_wide(a, b):
    a_high, a_low = halves(a)
    b_high, b_low = halves(b)
    both = dot(a_high, jnp.concatenate([b_high, b_low], axis=1), NN)
    return both[:, :RANK] + (both[:, RANK:] + dot(a_low, b_high, NN))


def dot_deep(a, b):
    a_high, a_low = halves(a)
    b_high, b_low = halves(b)
    both = jnp.concatenate([a_high, a_low], axis=1)
    return dot(both, jnp.concatenate([b_high, b_high], axis=1), NT) + dot(a_high, b_low, NT)


def left_kernel(other, place, gradient, feedback, prior, left, merged, gradient_in, feedback_in, prior_in, sems, prior_sem):
    del other, place
    steps = gradient_in.shape[0]
    rows = ROWS * MATRICES // steps
    per = steps // MATRICES

    def fetch(i):
        m, at = i // per, i % per * rows
        return (
            pltpu.make_async_copy(gradient.at[m, pl.ds(at, rows)], gradient_in.at[i], sems.at[0, i]),
            pltpu.make_async_copy(feedback.at[m, pl.ds(at, rows)], feedback_in.at[i], sems.at[1, i]),
        )

    def fetch_prior(m):
        return pltpu.make_async_copy(prior.at[m], prior_in.at[m], prior_sem.at[m])

    for i in range(steps):
        if i % per == 0:
            fetch_prior(i // per).start()
        for copy in fetch(i):
            copy.start()
    for i in range(steps):
        m, at = i // per, i % per * rows
        if at == 0:
            fetch_prior(m).wait()
        for copy in fetch(i):
            copy.wait()
        total = gradient_in[i].astype(f32) + feedback_in[i]
        merged[m, at : at + rows] = total
        left[at // CHUNK : (at + rows) // CHUNK, m] = dot_wide(total, prior_in[m]).reshape(rows // CHUNK, CHUNK, RANK)


def left_terms(other, place, gradient, feedback, right_prior, steps=4):
    rows = ROWS * MATRICES // steps
    return pl.pallas_call(
        left_kernel,
        in_specs=[pl.BlockSpec(memory_space=pltpu.SMEM)] * 2 + [pl.BlockSpec(memory_space=pltpu.HBM)] * 3,
        out_specs=[pl.BlockSpec(memory_space=pltpu.VMEM)] * 2,
        out_shape=[
            jax.ShapeDtypeStruct((ROWS // CHUNK, MATRICES, CHUNK, RANK), f32),
            jax.ShapeDtypeStruct((MATRICES, ROWS, WIDTH), f32),
        ],
        scratch_shapes=[
            pltpu.VMEM((steps, rows, WIDTH), bf16),
            pltpu.VMEM((steps, rows, WIDTH), f32),
            pltpu.VMEM((MATRICES, WIDTH, RANK), f32),
            pltpu.SemaphoreType.DMA((2, steps)),
            pltpu.SemaphoreType.DMA((MATRICES,)),
        ],
        compiler_params=pltpu.CompilerParams(vmem_limit_bytes=24 * MIB),
        name="left_terms",
    )(other, place, gradient, feedback, right_prior)


def stacked(left):
    return jnp.concatenate(halves(left), axis=1)


def gram_of(both):
    square = dot(both, both, TN)
    return square[:RANK, :RANK] + (square[RANK:, :RANK] + square[:RANK, RANK:] + square[RANK:, RANK:])


def right_kernel(which, merged, left_mean, right, *grams):
    i = which[0]
    both = stacked(left_mean[:, i].reshape(ROWS, RANK))
    if grams:
        grams[0][...] = gram_of(both)
        grams[1][...] = gram_of(stacked(left_mean[:, 1 - i].reshape(ROWS, RANK)))
    cols = WIDTH // 2
    for at in range(0, WIDTH, cols):
        merged_high, merged_low = halves(merged[i, :, at : at + cols])
        double = dot(both, merged_high, TN)
        total = double[:RANK] + (double[RANK:] + dot(both[:, :RANK], merged_low, TN))
        right[at : at + cols] = total.T


def right_terms(which, merged, left_mean, with_gram):
    square = jax.ShapeDtypeStruct((RANK, RANK), f32)
    return pl.pallas_call(
        right_kernel,
        in_specs=[pl.BlockSpec(memory_space=pltpu.SMEM)] + [pl.BlockSpec(memory_space=pltpu.VMEM)] * 2,
        out_shape=[jax.ShapeDtypeStruct((WIDTH, RANK), f32)] + [square] * (2 * with_gram),
        compiler_params=pltpu.CompilerParams(vmem_limit_bytes=24 * MIB),
        cost_estimate=pl.CostEstimate(flops=8 * 10**8, bytes_accessed=4 * 10**6, transcendentals=0),
        name="right_terms",
    )(which, merged, left_mean)


def tree_sum(terms):
    while len(terms) > 1:
        terms = [a + b for a, b in zip(terms[::2], terms[1::2])]
    return terms[0]


def inverse_kernel(gram, out):
    rows = lax.broadcasted_iota(jnp.int32, (RANK, RANK), 0)
    cols = lax.broadcasted_iota(jnp.int32, (RANK, RANK), 1)
    diagonal = rows == cols
    matrix = gram[...] * (1.0 / FEATURES)
    trace = jnp.sum(jnp.where(diagonal, matrix, 0.0))
    ridge = ridge_relative * (trace / RANK) + ridge_absolute
    matrix = jnp.where(diagonal, matrix + ridge, matrix)
    unit = jnp.where(diagonal, 1.0, 0.0)
    panels = RANK // 8
    left = [matrix[8 * q : 8 * q + 8] for q in range(panels)]
    right = [unit[8 * q : 8 * q + 8] for q in range(panels)]
    row = lax.broadcasted_iota(jnp.int32, (8, RANK), 0)

    def wide(x):
        return jnp.broadcast_to(x, (8, RANK))

    for p in range(panels):
        at = 8 * p
        col = [wide(left[p][:, at + j : at + j + 1]) for j in range(8)]
        solved_left, solved_right, reduced = left[p], right[p], right[p]
        pivots = scales = jnp.ones((8, RANK), f32)
        for j in range(8):
            pivot = wide(col[j][j : j + 1])
            scale = 1.0 / pivot
            factor = col[j] * scale
            below = jnp.where(row > j, factor, 0.0)
            beside = jnp.where(row != j, factor, 0.0)
            pivots = jnp.where(row == j, pivot, pivots)
            scales = jnp.where(row == j, scale, scales)
            row_left, row_right = wide(solved_left[j : j + 1]), wide(reduced[j : j + 1])
            for t in range(j + 1, 8):
                col[t] = col[t] - beside * wide(col[t][j : j + 1])
            solved_left = solved_left - beside * row_left
            solved_right = solved_right - beside * row_right
            reduced = reduced - below * row_right
        out[at : at + 8] = reduced * lax.rsqrt(pivots)
        solved_left, solved_right = solved_left * scales, solved_right * scales
        row_left = [wide(solved_left[j : j + 1]) for j in range(8)]
        row_right = [wide(solved_right[j : j + 1]) for j in range(8)]
        for q in range(p + 1, panels):
            col = [wide(left[q][:, at + j : at + j + 1]) for j in range(8)]
            left[q] = left[q] - tree_sum([c * r for c, r in zip(col, row_left)])
            right[q] = right[q] - tree_sum([c * r for c, r in zip(col, row_right)])


def inverse_factor(gram):
    return pl.pallas_call(
        inverse_kernel,
        out_shape=jax.ShapeDtypeStruct((RANK, RANK), f32),
        compiler_params=pltpu.CompilerParams(vmem_limit_bytes=16 * MIB),
        cost_estimate=pl.CostEstimate(flops=3 * 10**9, bytes_accessed=10**5, transcendentals=0),
        name="inverse_factor",
    )(gram)


def basis_kernel(core, left_mean, own, other, basis, operand, token):
    token[...] = jnp.zeros(token.shape, f32)
    for i, inverse in ((core[0], own), (1 - core[0], other)):
        rows = dot_wide(left_mean[:, i].reshape(ROWS, RANK), inverse[...].T)
        basis[i] = rows
        operand[i] = stacked(rows * (1.0 / math.sqrt(FEATURES)))


def basis_rows(core, left_mean, own, other):
    return pl.pallas_call(
        basis_kernel,
        in_specs=[pl.BlockSpec(memory_space=pltpu.SMEM)] + [pl.BlockSpec(memory_space=pltpu.VMEM)] * 3,
        out_shape=[
            jax.ShapeDtypeStruct((MATRICES, ROWS, RANK), f32),
            jax.ShapeDtypeStruct((MATRICES, ROWS, 2 * RANK), bf16),
            jax.ShapeDtypeStruct((8, RANK), f32),
        ],
        compiler_params=pltpu.CompilerParams(vmem_limit_bytes=16 * MIB),
        cost_estimate=pl.CostEstimate(flops=8 * 10**8, bytes_accessed=2 * 10**6, transcendentals=0),
        name="basis_rows",
    )(core, left_mean, own, other)


def factor_kernel(*refs):
    *parts, inverse, out = refs
    total = tree_sum([part[...] for part in parts])
    rows = dot_wide(total, inverse[...].T) * (1.0 / (32 * math.sqrt(FEATURES)))
    for i in range(out.shape[0]):
        out[i] = rows


def factor_rows(parts, inverse, copies):
    return pl.pallas_call(
        factor_kernel,
        out_shape=jax.ShapeDtypeStruct((copies,) + parts[0].shape, f32),
        compiler_params=pltpu.CompilerParams(vmem_limit_bytes=16 * MIB),
        cost_estimate=pl.CostEstimate(flops=10**8, bytes_accessed=4 * 10**5, transcendentals=0),
        name="factor_rows",
    )(*parts, inverse)


def tie_kernel(x, after, out):
    del x, after, out


def tie(x, after):
    return pl.pallas_call(
        tie_kernel,
        in_specs=[pl.BlockSpec(memory_space=pl.ANY), pl.BlockSpec(memory_space=pltpu.VMEM)],
        out_specs=pl.BlockSpec(memory_space=pl.ANY),
        out_shape=pltpu.VMEM(x.shape, x.dtype),
        input_output_aliases={0: 0},
        compiler_params=pltpu.CompilerParams(vmem_limit_bytes=MIB),
        name="tie",
    )(in_vmem(x), after)


def fetches(which, gradient, feedback, gradient_in, feedback_in, sems, i):
    rows = gradient_in.shape[1]
    at = pl.ds(i * rows, rows)
    return (
        pltpu.make_async_copy(gradient.at[which, at], gradient_in.at[i], sems.at[0, i]),
        pltpu.make_async_copy(feedback.at[which, at], feedback_in.at[i], sems.at[1, i]),
    )


def merge_arrived(which, gradient, feedback, gradient_in, feedback_in, sems, merged):
    steps, rows, _ = gradient_in.shape
    for i in range(steps):
        for copy in fetches(which, gradient, feedback, gradient_in, feedback_in, sems, i):
            copy.wait()
        merged[i * rows : (i + 1) * rows] = gradient_in[i].astype(f32) + feedback_in[i]


def fetch_scratch(steps):
    rows = ROWS // steps
    return [
        pltpu.VMEM((steps, rows, WIDTH), bf16),
        pltpu.VMEM((steps, rows, WIDTH), f32),
        pltpu.SemaphoreType.DMA((2, steps)),
    ]


def merge_kernel(which, gradient, feedback, after, merged, token, *scratch):
    del after
    token[...] = jnp.zeros(token.shape, f32)
    arrays = (which[0], gradient, feedback, *scratch)
    for i in range(scratch[0].shape[0]):
        for copy in fetches(*arrays, i):
            copy.start()
    merge_arrived(*arrays, merged)


def merge(which, gradient, feedback, after):
    return pl.pallas_call(
        merge_kernel,
        in_specs=[pl.BlockSpec(memory_space=pltpu.SMEM)]
        + [pl.BlockSpec(memory_space=pltpu.HBM)] * 2
        + [pl.BlockSpec(memory_space=pltpu.VMEM)],
        out_shape=[jax.ShapeDtypeStruct((ROWS, WIDTH), f32), jax.ShapeDtypeStruct((8, RANK), f32)],
        scratch_shapes=fetch_scratch(2),
        compiler_params=pltpu.CompilerParams(vmem_limit_bytes=16 * MIB),
        cost_estimate=pl.CostEstimate(flops=10**8, bytes_accessed=5 * 10**6, transcendentals=0),
        name="merge",
    )(which, gradient, feedback, after)


def finish_kernel(which, merged, operand, right, *rest):
    *rest, renewed_out, turned, sems = rest
    w = which[0]
    steps, rows, _ = renewed_out.shape
    if len(rest) > 4:
        gradient, feedback, renewed, factor, merged_next, *scratch = rest
        arrays = (1 - w, gradient, feedback, *scratch)
        for i in range(scratch[0].shape[0]):
            for copy in fetches(*arrays, i):
                copy.start()
    else:
        renewed, factor = rest[-2:]

    def store(i):
        return pltpu.make_async_copy(renewed_out.at[i], renewed.at[w, pl.ds(i * rows, rows)], sems.at[i])

    store_factor = pltpu.make_async_copy(right, factor.at[w], sems.at[steps])
    high, low = halves(right[...])
    turned[:, :RANK] = high
    turned[:, RANK : 2 * RANK] = high
    turned[:, 2 * RANK :] = low
    for i in range(steps):
        at = slice(i * rows, (i + 1) * rows)
        both = operand[w, at]
        approx = dot(both, turned[:, : 2 * RANK], NT) + dot(both[:, :RANK], turned[:, 2 * RANK :], NT)
        renewed_out[i] = merged[at] - approx
        store(i).start()
    store_factor.start()
    if len(rest) > 4:
        merge_arrived(*arrays, merged_next)
    for i in range(steps):
        store(i).wait()
    store_factor.wait()


def finish(which, merged, operand, right, ahead=(), before=(), steps=2):
    rows = ROWS // steps
    outs = [
        jax.ShapeDtypeStruct((MATRICES, ROWS, WIDTH), f32),
        jax.ShapeDtypeStruct((MATRICES, WIDTH, RANK), f32),
    ]
    return pl.pallas_call(
        finish_kernel,
        in_specs=[pl.BlockSpec(memory_space=pltpu.SMEM)]
        + [pl.BlockSpec(memory_space=pltpu.VMEM)] * 3
        + [pl.BlockSpec(memory_space=pltpu.HBM)] * len(ahead)
        + [pl.BlockSpec(memory_space=pl.ANY)] * len(before),
        out_specs=[pl.BlockSpec(memory_space=pl.ANY)] * 2 + [pl.BlockSpec(memory_space=pltpu.VMEM)] * bool(ahead),
        out_shape=outs + [jax.ShapeDtypeStruct((ROWS, WIDTH), f32)] * bool(ahead),
        scratch_shapes=fetch_scratch(2) * bool(ahead)
        + [
            pltpu.VMEM((steps, rows, WIDTH), f32),
            pltpu.VMEM((WIDTH, 3 * RANK), bf16),
            pltpu.SemaphoreType.DMA((steps + 1,)),
        ],
        input_output_aliases={4: 0, 5: 1} if before else {},
        compiler_params=pltpu.CompilerParams(vmem_limit_bytes=24 * MIB),
        cost_estimate=pl.CostEstimate(flops=8 * 10**8, bytes_accessed=6 * 10**6, transcendentals=0),
        name="finish",
    )(which, merged, operand, right, *ahead, *before)


def share_kernel(*refs, scale, count):
    parts, out = refs[:count], refs[-1]
    if count == 1:
        parts = [parts[0][i] for i in range(parts[0].shape[0])]
    else:
        parts = [part[0] for part in parts]
    total = tree_sum(parts) * scale
    for i in range(out.shape[0]):
        out[i] = total


def share(parts, copies, scale, after=()):
    parts = parts if isinstance(parts, list) else [parts]
    return pl.pallas_call(
        functools.partial(share_kernel, scale=scale, count=len(parts)),
        out_shape=jax.ShapeDtypeStruct((copies,) + parts[0].shape[1:], f32),
        compiler_params=pltpu.CompilerParams(vmem_limit_bytes=8 * MIB),
        name="share",
    )(*parts, *after)


def parcel_kernel(place, right, right_other, gram, gram_other, out, gram_sum):
    gram_sum[...] = gram[...] + gram_other[...]
    piece = gram_sum[pl.ds(pl.multiple_of(place[0] * PIECE, PIECE), PIECE)]
    for i in range(BOX):
        at = slice(i * SHARE, (i + 1) * SHARE)
        out[i, :SHARE] = right[at] + right_other[at]
        out[i, SHARE:] = piece


def parcels(place, right, right_other, gram, gram_other):
    return pl.pallas_call(
        parcel_kernel,
        in_specs=[pl.BlockSpec(memory_space=pltpu.SMEM)] + [pl.BlockSpec(memory_space=pltpu.VMEM)] * 4,
        out_shape=jax.ShapeDtypeStruct((BOX, SHARE + PIECE, RANK), f32),
        scratch_shapes=[pltpu.VMEM((RANK, RANK), f32)],
        compiler_params=pltpu.CompilerParams(vmem_limit_bytes=8 * MIB),
        name="parcels",
    )(place, right, right_other, gram, gram_other)


def unpack_kernel(parts, total, gram):
    total[...] = tree_sum([parts[i, :SHARE] for i in range(BOX)])
    for k in range(RANK // PIECE):
        gram[k * PIECE : (k + 1) * PIECE] = tree_sum([parts[4 * k + x, SHARE:] for x in range(4)])


def unpack(parts):
    return pl.pallas_call(
        unpack_kernel,
        out_shape=[jax.ShapeDtypeStruct((SHARE, RANK), f32), jax.ShapeDtypeStruct((RANK, RANK), f32)],
        compiler_params=pltpu.CompilerParams(vmem_limit_bytes=8 * MIB),
        name="unpack",
    )(parts)


def exchange(x, axes):
    return lax.all_to_all(x, axes, 0, 0, tiled=True)


def swap(x):
    return lax.ppermute(x, "core", [(0, 1), (1, 0)])


def rounds(x, axis):
    return [x] + [lax.ppermute(x, axis, [(i, (i + s) % 4) for i in range(4)]) for s in (1, 3, 2)]


def shards(gradient, feedback, right_prior):
    own = lax.axis_index("core")[None]
    other = 1 - own
    place = lax.axis_index(("zl", "y"))[None]
    column, box = ("zl", "y"), ("zl", "y", "x")
    gradient, feedback, right_prior = in_hbm(gradient[0]), in_hbm(feedback[0]), in_hbm(right_prior)
    left, merged = left_terms(other, place, gradient, feedback, right_prior)
    left = rounds(share(exchange(left, column), 1, 1.0 / 32), "zh")
    left_mean = exchange(share(left, 8, 1.0), column)

    right_other, gram_other, gram = right_terms(other, merged, left_mean, True)
    right_other, gram_other = swap(right_other), swap(gram_other)
    right = right_terms(own, merged, left_mean, False)[0]
    parts = exchange(parcels(place, right, right_other, gram, gram_other), box)
    total, gram = unpack(parts)
    totals = rounds(total, "zh")
    inverse = inverse_factor(gram)
    right = exchange(factor_rows(totals, inverse, 32), box).reshape(WIDTH, RANK)
    basis, operand, token = basis_rows(own, left_mean, inverse, swap(inverse))
    merged, token = merge(own, gradient, feedback, token)
    right = tie(right, token)

    *done, merged = finish(own, merged, operand, right, (gradient, feedback))
    renewed, factor = finish(other, merged, operand, swap(right), (), tuple(done))
    return renewed[None], basis, factor


def solution(mesh):
    chips = Mesh(mesh.devices.reshape(4, 2, 4, 4, 2), ("zh", "zl", "y", "x", "core"))
    rep, fsdp = ("zh", "zl", "y"), ("x", "core")
    in_specs = (P(rep, None, fsdp, None), P(rep, None, fsdp, None), P())
    out_specs = (P(rep, None, fsdp, None), P(None, fsdp, None), P())
    return jax.shard_map(shards, mesh=chips, in_specs=in_specs, out_specs=out_specs, check_vma=False)
```

```python
import functools
import math

import jax
import jax.numpy as jnp
from jax import lax
from jax.experimental import pallas as pl
from jax.experimental.pallas import tpu as pltpu
from jax.sharding import Mesh, PartitionSpec as P

FEATURES = 4096
WIDTH = 1024
RANK = 128
MATRICES = 2
ROWS = 512
CHUNK = 64
BOX = 32
SHARE = WIDTH // BOX
PIECE = 16
ridge_relative = 0.001
ridge_absolute = 1e-06
MIB = 1 << 20
f32 = jnp.float32
bf16 = jnp.bfloat16


def halves(x):
    high = x.astype(bf16)
    return high, (x - high.astype(f32)).astype(bf16)


def dot(a, b, dims):
    return lax.dot_general(a, b, (dims, ((), ())), preferred_element_type=f32)


def in_vmem(x):
    return pltpu.with_memory_space_constraint(x, pltpu.VMEM)


def in_hbm(x):
    return pltpu.with_memory_space_constraint(x, pltpu.HBM)


NN = ((1,), (0,))
NT = ((1,), (1,))
TN = ((0,), (0,))


def dot_wide(a, b):
    a_high, a_low = halves(a)
    b_high, b_low = halves(b)
    both = dot(a_high, jnp.concatenate([b_high, b_low], axis=1), NN)
    return both[:, :RANK] + (both[:, RANK:] + dot(a_low, b_high, NN))


def dot_deep(a, b):
    a_high, a_low = halves(a)
    b_high, b_low = halves(b)
    both = jnp.concatenate([a_high, a_low], axis=1)
    return dot(both, jnp.concatenate([b_high, b_high], axis=1), NT) + dot(a_high, b_low, NT)


def left_kernel(other, place, gradient, feedback, prior, left, merged, gradient_in, feedback_in, prior_in, sems, prior_sem):
    del other, place
    steps = gradient_in.shape[0]
    rows = ROWS * MATRICES // steps
    per = steps // MATRICES

    def fetch(i):
        m, at = i // per, i % per * rows
        return (
            pltpu.make_async_copy(gradient.at[m, pl.ds(at, rows)], gradient_in.at[i], sems.at[0, i]),
            pltpu.make_async_copy(feedback.at[m, pl.ds(at, rows)], feedback_in.at[i], sems.at[1, i]),
        )

    def fetch_prior(m):
        return pltpu.make_async_copy(prior.at[m], prior_in.at[m], prior_sem.at[m])

    for i in range(steps):
        if i % per == 0:
            fetch_prior(i // per).start()
        for copy in fetch(i):
            copy.start()
    for i in range(steps):
        m, at = i // per, i % per * rows
        if at == 0:
            fetch_prior(m).wait()
        for copy in fetch(i):
            copy.wait()
        total = gradient_in[i].astype(f32) + feedback_in[i]
        merged[m, at : at + rows] = total
        left[at // CHUNK : (at + rows) // CHUNK, m] = dot_wide(total, prior_in[m]).reshape(rows // CHUNK, CHUNK, RANK)


def left_terms(other, place, gradient, feedback, right_prior, steps=4):
    rows = ROWS * MATRICES // steps
    return pl.pallas_call(
        left_kernel,
        in_specs=[pl.BlockSpec(memory_space=pltpu.SMEM)] * 2 + [pl.BlockSpec(memory_space=pltpu.HBM)] * 3,
        out_specs=[pl.BlockSpec(memory_space=pltpu.VMEM)] * 2,
        out_shape=[
            jax.ShapeDtypeStruct((ROWS // CHUNK, MATRICES, CHUNK, RANK), f32),
            jax.ShapeDtypeStruct((MATRICES, ROWS, WIDTH), f32),
        ],
        scratch_shapes=[
            pltpu.VMEM((steps, rows, WIDTH), bf16),
            pltpu.VMEM((steps, rows, WIDTH), f32),
            pltpu.VMEM((MATRICES, WIDTH, RANK), f32),
            pltpu.SemaphoreType.DMA((2, steps)),
            pltpu.SemaphoreType.DMA((MATRICES,)),
        ],
        compiler_params=pltpu.CompilerParams(vmem_limit_bytes=24 * MIB),
        name="left_terms",
    )(other, place, gradient, feedback, right_prior)


def stacked(left):
    return jnp.concatenate(halves(left), axis=1)


def gram_of(both):
    square = dot(both, both, TN)
    return square[:RANK, :RANK] + (square[RANK:, :RANK] + square[:RANK, RANK:] + square[RANK:, RANK:])


def right_kernel(which, merged, left_mean, right, *grams):
    i = which[0]
    both = stacked(left_mean[:, i].reshape(ROWS, RANK))
    if grams:
        grams[0][...] = gram_of(both)
        grams[1][...] = gram_of(stacked(left_mean[:, 1 - i].reshape(ROWS, RANK)))
    cols = WIDTH // 2
    for at in range(0, WIDTH, cols):
        merged_high, merged_low = halves(merged[i, :, at : at + cols])
        double = dot(both, merged_high, TN)
        total = double[:RANK] + (double[RANK:] + dot(both[:, :RANK], merged_low, TN))
        right[at : at + cols] = total.T


def right_terms(which, merged, left_mean, with_gram):
    square = jax.ShapeDtypeStruct((RANK, RANK), f32)
    return pl.pallas_call(
        right_kernel,
        in_specs=[pl.BlockSpec(memory_space=pltpu.SMEM)] + [pl.BlockSpec(memory_space=pltpu.VMEM)] * 2,
        out_shape=[jax.ShapeDtypeStruct((WIDTH, RANK), f32)] + [square] * (2 * with_gram),
        compiler_params=pltpu.CompilerParams(vmem_limit_bytes=24 * MIB),
        cost_estimate=pl.CostEstimate(flops=8 * 10**8, bytes_accessed=4 * 10**6, transcendentals=0),
        name="right_terms",
    )(which, merged, left_mean)


def tree_sum(terms):
    while len(terms) > 1:
        terms = [a + b for a, b in zip(terms[::2], terms[1::2])]
    return terms[0]


def inverse_kernel(gram, out):
    rows = lax.broadcasted_iota(jnp.int32, (RANK, RANK), 0)
    cols = lax.broadcasted_iota(jnp.int32, (RANK, RANK), 1)
    diagonal = rows == cols
    matrix = gram[...] * (1.0 / FEATURES)
    trace = jnp.sum(jnp.where(diagonal, matrix, 0.0))
    ridge = ridge_relative * (trace / RANK) + ridge_absolute
    matrix = jnp.where(diagonal, matrix + ridge, matrix)
    panels = RANK // 8
    left = [matrix[8 * q : 8 * q + 8] for q in range(panels)]
    row = lax.broadcasted_iota(jnp.int32, (8, RANK), 0)
    lane = lax.broadcasted_iota(jnp.int32, (8, RANK), 1)

    def wide(x):
        return jnp.broadcast_to(x, (8, RANK))

    for p in range(panels):
        at = 8 * p
        here = (lane >= at) & (lane < at + 8)
        col = [wide(left[p][:, at + j : at + j + 1]) for j in range(8)]
        solved = reduced = jnp.where(here, jnp.where(lane - at == row, 1.0, 0.0), left[p])
        pivots = same = beside = jnp.ones((8, RANK), f32)
        for j in range(0, 8, 2):
            a, b, d = wide(col[j][j : j + 1]), wide(col[j + 1][j : j + 1]), wide(col[j + 1][j + 1 : j + 2])
            det = a * d - b * b
            scale = 1.0 / det
            first, second = row == j, row == j + 1
            away = (row < j) | (row > j + 1)
            factor_0 = jnp.where(away, col[j] * d - col[j + 1] * b, 0.0) * scale
            factor_1 = jnp.where(away, col[j + 1] * a - col[j] * b, 0.0) * scale
            for t in range(j + 2, 8):
                col[t] = col[t] - (factor_0 * wide(col[t][j : j + 1]) + factor_1 * wide(col[t][j + 1 : j + 2]))
            row_0, row_1 = wide(reduced[j : j + 1]), wide(reduced[j + 1 : j + 2])
            scale_a = 1.0 / a
            change = factor_0 * row_0 + factor_1 * row_1
            solved = solved - change
            reduced = reduced - jnp.where(row > j + 1, change, jnp.where(second, (b * scale_a) * row_0, 0.0))
            pivots = jnp.where(first, a, jnp.where(second, det * scale_a, pivots))
            same = jnp.where(first, d * scale, jnp.where(second, a * scale, same))
            beside = jnp.where(first | second, -(b * scale), beside)
        out[at : at + 8] = jnp.where(lane < at + 8, reduced * lax.rsqrt(pivots), 0.0)
        if p + 1 == panels:
            break
        partner = jnp.where(
            row % 2 == 0,
            jnp.concatenate([solved[1:], solved[:1]], axis=0),
            jnp.concatenate([solved[7:], solved[:7]], axis=0),
        )
        solved = same * solved + beside * partner
        pieces = [wide(solved[j : j + 1]) for j in range(8)]
        for q in range(p + 1, panels):
            terms = [wide(left[q][:, at + j : at + j + 1]) * pieces[j] for j in range(8)]
            left[q] = jnp.where(here, 0.0, left[q]) - tree_sum(terms)


def inverse_factor(gram):
    return pl.pallas_call(
        inverse_kernel,
        out_shape=jax.ShapeDtypeStruct((RANK, RANK), f32),
        compiler_params=pltpu.CompilerParams(vmem_limit_bytes=16 * MIB),
        cost_estimate=pl.CostEstimate(flops=3 * 10**9, bytes_accessed=10**5, transcendentals=0),
        name="inverse_factor",
    )(gram)


def basis_kernel(core, left_mean, own, other, basis, operand, token):
    token[...] = jnp.zeros(token.shape, f32)
    for i, inverse in ((core[0], own), (1 - core[0], other)):
        rows = dot_wide(left_mean[:, i].reshape(ROWS, RANK), inverse[...].T)
        basis[i] = rows
        operand[i] = stacked(rows * (1.0 / math.sqrt(FEATURES)))


def basis_rows(core, left_mean, own, other):
    return pl.pallas_call(
        basis_kernel,
        in_specs=[pl.BlockSpec(memory_space=pltpu.SMEM)] + [pl.BlockSpec(memory_space=pltpu.VMEM)] * 3,
        out_shape=[
            jax.ShapeDtypeStruct((MATRICES, ROWS, RANK), f32),
            jax.ShapeDtypeStruct((MATRICES, ROWS, 2 * RANK), bf16),
            jax.ShapeDtypeStruct((8, RANK), f32),
        ],
        compiler_params=pltpu.CompilerParams(vmem_limit_bytes=16 * MIB),
        cost_estimate=pl.CostEstimate(flops=8 * 10**8, bytes_accessed=2 * 10**6, transcendentals=0),
        name="basis_rows",
    )(core, left_mean, own, other)


def factor_kernel(*refs):
    *parts, inverse, out = refs
    total = tree_sum([part[...] for part in parts])
    rows = dot_wide(total, inverse[...].T) * (1.0 / (32 * math.sqrt(FEATURES)))
    for i in range(out.shape[0]):
        out[i] = rows


def factor_rows(parts, inverse, copies):
    return pl.pallas_call(
        factor_kernel,
        out_shape=jax.ShapeDtypeStruct((copies,) + parts[0].shape, f32),
        compiler_params=pltpu.CompilerParams(vmem_limit_bytes=16 * MIB),
        cost_estimate=pl.CostEstimate(flops=10**8, bytes_accessed=4 * 10**5, transcendentals=0),
        name="factor_rows",
    )(*parts, inverse)


def tie_kernel(x, after, out):
    del x, after, out


def tie(x, after):
    return pl.pallas_call(
        tie_kernel,
        in_specs=[pl.BlockSpec(memory_space=pl.ANY), pl.BlockSpec(memory_space=pltpu.VMEM)],
        out_specs=pl.BlockSpec(memory_space=pl.ANY),
        out_shape=pltpu.VMEM(x.shape, x.dtype),
        input_output_aliases={0: 0},
        compiler_params=pltpu.CompilerParams(vmem_limit_bytes=MIB),
        name="tie",
    )(in_vmem(x), after)


def fetches(which, gradient, feedback, gradient_in, feedback_in, sems, i):
    rows = gradient_in.shape[1]
    at = pl.ds(i * rows, rows)
    return (
        pltpu.make_async_copy(gradient.at[which, at], gradient_in.at[i], sems.at[0, i]),
        pltpu.make_async_copy(feedback.at[which, at], feedback_in.at[i], sems.at[1, i]),
    )


def merge_arrived(which, gradient, feedback, gradient_in, feedback_in, sems, merged):
    steps, rows, _ = gradient_in.shape
    for i in range(steps):
        for copy in fetches(which, gradient, feedback, gradient_in, feedback_in, sems, i):
            copy.wait()
        merged[i * rows : (i + 1) * rows] = gradient_in[i].astype(f32) + feedback_in[i]


def fetch_scratch(steps):
    rows = ROWS // steps
    return [
        pltpu.VMEM((steps, rows, WIDTH), bf16),
        pltpu.VMEM((steps, rows, WIDTH), f32),
        pltpu.SemaphoreType.DMA((2, steps)),
    ]


def merge_kernel(which, gradient, feedback, after, merged, token, *scratch):
    del after
    token[...] = jnp.zeros(token.shape, f32)
    arrays = (which[0], gradient, feedback, *scratch)
    for i in range(scratch[0].shape[0]):
        for copy in fetches(*arrays, i):
            copy.start()
    merge_arrived(*arrays, merged)


def merge(which, gradient, feedback, after):
    return pl.pallas_call(
        merge_kernel,
        in_specs=[pl.BlockSpec(memory_space=pltpu.SMEM)]
        + [pl.BlockSpec(memory_space=pltpu.HBM)] * 2
        + [pl.BlockSpec(memory_space=pltpu.VMEM)],
        out_shape=[jax.ShapeDtypeStruct((ROWS, WIDTH), f32), jax.ShapeDtypeStruct((8, RANK), f32)],
        scratch_shapes=fetch_scratch(2),
        compiler_params=pltpu.CompilerParams(vmem_limit_bytes=16 * MIB),
        cost_estimate=pl.CostEstimate(flops=10**8, bytes_accessed=5 * 10**6, transcendentals=0),
        name="merge",
    )(which, gradient, feedback, after)


def finish_kernel(which, merged, operand, right, *rest):
    *rest, renewed_out, turned, sems = rest
    w = which[0]
    steps, rows, _ = renewed_out.shape
    if len(rest) > 4:
        gradient, feedback, renewed, factor, merged_next, *scratch = rest
        arrays = (1 - w, gradient, feedback, *scratch)
        for i in range(scratch[0].shape[0]):
            for copy in fetches(*arrays, i):
                copy.start()
    else:
        renewed, factor = rest[-2:]

    def store(i):
        return pltpu.make_async_copy(renewed_out.at[i], renewed.at[w, pl.ds(i * rows, rows)], sems.at[i])

    store_factor = pltpu.make_async_copy(right, factor.at[w], sems.at[steps])
    store_factor.start()
    high, low = halves(right[...])
    turned[:, :RANK] = high
    turned[:, RANK : 2 * RANK] = high
    turned[:, 2 * RANK :] = low
    for i in range(steps):
        at = slice(i * rows, (i + 1) * rows)
        both = operand[w, at]
        approx = dot(both, turned[:, : 2 * RANK], NT) + dot(both[:, :RANK], turned[:, 2 * RANK :], NT)
        renewed_out[i] = merged[at] - approx
        store(i).start()
    if len(rest) > 4:
        merge_arrived(*arrays, merged_next)
    for i in range(steps):
        store(i).wait()
    store_factor.wait()


def finish(which, merged, operand, right, ahead=(), before=(), steps=2):
    rows = ROWS // steps
    outs = [
        jax.ShapeDtypeStruct((MATRICES, ROWS, WIDTH), f32),
        jax.ShapeDtypeStruct((MATRICES, WIDTH, RANK), f32),
    ]
    return pl.pallas_call(
        finish_kernel,
        in_specs=[pl.BlockSpec(memory_space=pltpu.SMEM)]
        + [pl.BlockSpec(memory_space=pltpu.VMEM)] * 3
        + [pl.BlockSpec(memory_space=pltpu.HBM)] * len(ahead)
        + [pl.BlockSpec(memory_space=pl.ANY)] * len(before),
        out_specs=[pl.BlockSpec(memory_space=pl.ANY)] * 2 + [pl.BlockSpec(memory_space=pltpu.VMEM)] * bool(ahead),
        out_shape=outs + [jax.ShapeDtypeStruct((ROWS, WIDTH), f32)] * bool(ahead),
        scratch_shapes=fetch_scratch(2) * bool(ahead)
        + [
            pltpu.VMEM((steps, rows, WIDTH), f32),
            pltpu.VMEM((WIDTH, 3 * RANK), bf16),
            pltpu.SemaphoreType.DMA((steps + 1,)),
        ],
        input_output_aliases={4: 0, 5: 1} if before else {},
        compiler_params=pltpu.CompilerParams(vmem_limit_bytes=24 * MIB),
        cost_estimate=pl.CostEstimate(flops=8 * 10**8, bytes_accessed=6 * 10**6, transcendentals=0),
        name="finish",
    )(which, merged, operand, right, *ahead, *before)


def share_kernel(*refs, scale, count):
    parts, out = refs[:count], refs[-1]
    if count == 1:
        parts = [parts[0][i] for i in range(parts[0].shape[0])]
    else:
        parts = [part[0] for part in parts]
    total = tree_sum(parts) * scale
    for i in range(out.shape[0]):
        out[i] = total


def share(parts, copies, scale, after=()):
    parts = parts if isinstance(parts, list) else [parts]
    return pl.pallas_call(
        functools.partial(share_kernel, scale=scale, count=len(parts)),
        out_shape=jax.ShapeDtypeStruct((copies,) + parts[0].shape[1:], f32),
        compiler_params=pltpu.CompilerParams(vmem_limit_bytes=8 * MIB),
        name="share",
    )(*parts, *after)


def parcel_kernel(place, right, right_other, gram, gram_other, out, gram_sum):
    gram_sum[...] = gram[...] + gram_other[...]
    piece = gram_sum[pl.ds(pl.multiple_of(place[0] * PIECE, PIECE), PIECE)]
    for i in range(BOX):
        at = slice(i * SHARE, (i + 1) * SHARE)
        out[i, :SHARE] = right[at] + right_other[at]
        out[i, SHARE:] = piece


def parcels(place, right, right_other, gram, gram_other):
    return pl.pallas_call(
        parcel_kernel,
        in_specs=[pl.BlockSpec(memory_space=pltpu.SMEM)] + [pl.BlockSpec(memory_space=pltpu.VMEM)] * 4,
        out_shape=jax.ShapeDtypeStruct((BOX, SHARE + PIECE, RANK), f32),
        scratch_shapes=[pltpu.VMEM((RANK, RANK), f32)],
        compiler_params=pltpu.CompilerParams(vmem_limit_bytes=8 * MIB),
        name="parcels",
    )(place, right, right_other, gram, gram_other)


def unpack_kernel(parts, total, gram):
    total[...] = tree_sum([parts[i, :SHARE] for i in range(BOX)])
    for k in range(RANK // PIECE):
        gram[k * PIECE : (k + 1) * PIECE] = tree_sum([parts[4 * k + x, SHARE:] for x in range(4)])


def unpack(parts):
    return pl.pallas_call(
        unpack_kernel,
        out_shape=[jax.ShapeDtypeStruct((SHARE, RANK), f32), jax.ShapeDtypeStruct((RANK, RANK), f32)],
        compiler_params=pltpu.CompilerParams(vmem_limit_bytes=8 * MIB),
        name="unpack",
    )(parts)


def exchange(x, axes):
    return lax.all_to_all(x, axes, 0, 0, tiled=True)


def swap(x):
    return lax.ppermute(x, "core", [(0, 1), (1, 0)])


def rounds(x, axis):
    return [x] + [lax.ppermute(x, axis, [(i, (i + s) % 4) for i in range(4)]) for s in (1, 3, 2)]


def shards(gradient, feedback, right_prior):
    own = lax.axis_index("core")[None]
    other = 1 - own
    place = lax.axis_index(("zl", "y"))[None]
    column, box = ("zl", "y"), ("zl", "y", "x")
    gradient, feedback, right_prior = in_hbm(gradient[0]), in_hbm(feedback[0]), in_hbm(right_prior)
    left, merged = left_terms(other, place, gradient, feedback, right_prior)
    left = rounds(share(exchange(left, column), 1, 1.0 / 32), "zh")
    left_mean = exchange(share(left, 8, 1.0), column)

    right_other, gram_other, gram = right_terms(other, merged, left_mean, True)
    right_other, gram_other = swap(right_other), swap(gram_other)
    right = right_terms(own, merged, left_mean, False)[0]
    parts = exchange(parcels(place, right, right_other, gram, gram_other), box)
    total, gram = unpack(parts)
    totals = rounds(total, "zh")
    inverse = inverse_factor(gram)
    right = exchange(factor_rows(totals, inverse, 32), box).reshape(WIDTH, RANK)
    basis, operand, token = basis_rows(own, left_mean, inverse, swap(inverse))
    merged, token = merge(own, gradient, feedback, token)
    right = tie(right, token)

    *done, merged = finish(own, merged, operand, right, (gradient, feedback))
    renewed, factor = finish(other, merged, operand, swap(right), (), tuple(done))
    return renewed[None], basis, factor


def solution(mesh):
    chips = Mesh(mesh.devices.reshape(4, 2, 4, 4, 2), ("zh", "zl", "y", "x", "core"))
    rep, fsdp = ("zh", "zl", "y"), ("x", "core")
    in_specs = (P(rep, None, fsdp, None), P(rep, None, fsdp, None), P())
    out_specs = (P(rep, None, fsdp, None), P(None, fsdp, None), P())
    return jax.shard_map(shards, mesh=chips, in_specs=in_specs, out_specs=out_specs, check_vma=False)
```

```python
import functools
import math

import jax
import jax.numpy as jnp
from jax import lax
from jax.experimental import pallas as pl
from jax.experimental.pallas import tpu as pltpu
from jax.sharding import Mesh, PartitionSpec as P

FEATURES = 4096
WIDTH = 1024
RANK = 128
MATRICES = 2
ROWS = 512
CHUNK = 64
BOX = 32
SHARE = WIDTH // BOX
PIECE = 16
ridge_relative = 0.001
ridge_absolute = 1e-06
MIB = 1 << 20
f32 = jnp.float32
bf16 = jnp.bfloat16


def halves(x):
    high = x.astype(bf16)
    return high, (x - high.astype(f32)).astype(bf16)


def dot(a, b, dims):
    return lax.dot_general(a, b, (dims, ((), ())), preferred_element_type=f32)


def in_vmem(x):
    return pltpu.with_memory_space_constraint(x, pltpu.VMEM)


def in_hbm(x):
    return pltpu.with_memory_space_constraint(x, pltpu.HBM)


NN = ((1,), (0,))
NT = ((1,), (1,))
TN = ((0,), (0,))


def dot_wide(a, b):
    a_high, a_low = halves(a)
    b_high, b_low = halves(b)
    both = dot(a_high, jnp.concatenate([b_high, b_low], axis=1), NN)
    return both[:, :RANK] + (both[:, RANK:] + dot(a_low, b_high, NN))


def dot_deep(a, b):
    a_high, a_low = halves(a)
    b_high, b_low = halves(b)
    both = jnp.concatenate([a_high, a_low], axis=1)
    return dot(both, jnp.concatenate([b_high, b_high], axis=1), NT) + dot(a_high, b_low, NT)


def left_kernel(other, place, gradient, feedback, prior, left, merged, gradient_in, feedback_in, prior_in, sems, prior_sem):
    del other, place
    steps = gradient_in.shape[0]
    rows = ROWS * MATRICES // steps
    per = steps // MATRICES

    def fetch(i):
        m, at = i // per, i % per * rows
        return (
            pltpu.make_async_copy(gradient.at[m, pl.ds(at, rows)], gradient_in.at[i], sems.at[0, i]),
            pltpu.make_async_copy(feedback.at[m, pl.ds(at, rows)], feedback_in.at[i], sems.at[1, i]),
        )

    def fetch_prior(m):
        return pltpu.make_async_copy(prior.at[m], prior_in.at[m], prior_sem.at[m])

    for i in range(steps):
        if i % per == 0:
            fetch_prior(i // per).start()
        for copy in fetch(i):
            copy.start()
    for i in range(steps):
        m, at = i // per, i % per * rows
        if at == 0:
            fetch_prior(m).wait()
        for copy in fetch(i):
            copy.wait()
        total = gradient_in[i].astype(f32) + feedback_in[i]
        merged[m, at : at + rows] = total
        left[at // CHUNK : (at + rows) // CHUNK, m] = dot_wide(total, prior_in[m]).reshape(rows // CHUNK, CHUNK, RANK)


def left_terms(other, place, gradient, feedback, right_prior, steps=2):
    rows = ROWS * MATRICES // steps
    return pl.pallas_call(
        left_kernel,
        in_specs=[pl.BlockSpec(memory_space=pltpu.SMEM)] * 2 + [pl.BlockSpec(memory_space=pltpu.HBM)] * 3,
        out_specs=[pl.BlockSpec(memory_space=pltpu.VMEM)] * 2,
        out_shape=[
            jax.ShapeDtypeStruct((ROWS // CHUNK, MATRICES, CHUNK, RANK), f32),
            jax.ShapeDtypeStruct((MATRICES, ROWS, WIDTH), f32),
        ],
        scratch_shapes=[
            pltpu.VMEM((steps, rows, WIDTH), bf16),
            pltpu.VMEM((steps, rows, WIDTH), f32),
            pltpu.VMEM((MATRICES, WIDTH, RANK), f32),
            pltpu.SemaphoreType.DMA((2, steps)),
            pltpu.SemaphoreType.DMA((MATRICES,)),
        ],
        compiler_params=pltpu.CompilerParams(vmem_limit_bytes=24 * MIB),
        name="left_terms",
    )(other, place, gradient, feedback, right_prior)


def stacked(left):
    return jnp.concatenate(halves(left), axis=1)


def gram_of(both):
    square = dot(both, both, TN)
    return square[:RANK, :RANK] + (square[RANK:, :RANK] + square[:RANK, RANK:] + square[RANK:, RANK:])


def right_kernel(which, merged, left_mean, right, *gram):
    i = which[0]
    both = stacked(left_mean[:, i].reshape(ROWS, RANK))
    if gram:
        right[WIDTH:] = gram_of(both)
        gram[0][...] = gram_of(stacked(left_mean[:, 1 - i].reshape(ROWS, RANK)))
    cols = WIDTH // 2
    for at in range(0, WIDTH, cols):
        merged_high, merged_low = halves(merged[i, :, at : at + cols])
        double = dot(both, merged_high, TN)
        total = double[:RANK] + (double[RANK:] + dot(both[:, :RANK], merged_low, TN))
        right[at : at + cols] = total.T


def right_terms(which, merged, left_mean, with_gram):
    return pl.pallas_call(
        right_kernel,
        in_specs=[pl.BlockSpec(memory_space=pltpu.SMEM)] + [pl.BlockSpec(memory_space=pltpu.VMEM)] * 2,
        out_shape=[jax.ShapeDtypeStruct((WIDTH + RANK * with_gram, RANK), f32)]
        + [jax.ShapeDtypeStruct((RANK, RANK), f32)] * with_gram,
        compiler_params=pltpu.CompilerParams(vmem_limit_bytes=24 * MIB),
        cost_estimate=pl.CostEstimate(flops=8 * 10**8, bytes_accessed=4 * 10**6, transcendentals=0),
        name="right_terms",
    )(which, merged, left_mean)


def tree_sum(terms):
    while len(terms) > 1:
        terms = [a + b for a, b in zip(terms[::2], terms[1::2])]
    return terms[0]


def inverse_kernel(gram, out):
    rows = lax.broadcasted_iota(jnp.int32, (RANK, RANK), 0)
    cols = lax.broadcasted_iota(jnp.int32, (RANK, RANK), 1)
    diagonal = rows == cols
    matrix = gram[...] * (1.0 / FEATURES)
    trace = jnp.sum(jnp.where(diagonal, matrix, 0.0))
    ridge = ridge_relative * (trace / RANK) + ridge_absolute
    matrix = jnp.where(diagonal, matrix + ridge, matrix)
    panels = RANK // 8
    left = [matrix[8 * q : 8 * q + 8] for q in range(panels)]
    row = lax.broadcasted_iota(jnp.int32, (8, RANK), 0)
    lane = lax.broadcasted_iota(jnp.int32, (8, RANK), 1)

    def wide(x):
        return jnp.broadcast_to(x, (8, RANK))

    for p in range(panels):
        at = 8 * p
        here = (lane >= at) & (lane < at + 8)
        col = [wide(left[p][:, at + j : at + j + 1]) for j in range(8)]
        solved = reduced = jnp.where(here, jnp.where(lane - at == row, 1.0, 0.0), left[p])
        pivots = same = beside = jnp.ones((8, RANK), f32)
        for j in range(0, 8, 2):
            a, b, d = wide(col[j][j : j + 1]), wide(col[j + 1][j : j + 1]), wide(col[j + 1][j + 1 : j + 2])
            det = a * d - b * b
            scale = 1.0 / det
            first, second = row == j, row == j + 1
            away = (row < j) | (row > j + 1)
            factor_0 = jnp.where(away, col[j] * d - col[j + 1] * b, 0.0) * scale
            factor_1 = jnp.where(away, col[j + 1] * a - col[j] * b, 0.0) * scale
            for t in range(j + 2, 8):
                col[t] = col[t] - (factor_0 * wide(col[t][j : j + 1]) + factor_1 * wide(col[t][j + 1 : j + 2]))
            row_0, row_1 = wide(reduced[j : j + 1]), wide(reduced[j + 1 : j + 2])
            scale_a = 1.0 / a
            change = factor_0 * row_0 + factor_1 * row_1
            solved = solved - change
            reduced = reduced - jnp.where(row > j + 1, change, jnp.where(second, (b * scale_a) * row_0, 0.0))
            pivots = jnp.where(first, a, jnp.where(second, det * scale_a, pivots))
            same = jnp.where(first, d * scale, jnp.where(second, a * scale, same))
            beside = jnp.where(first | second, -(b * scale), beside)
        out[at : at + 8] = jnp.where(lane < at + 8, reduced * lax.rsqrt(pivots), 0.0)
        if p + 1 == panels:
            break
        partner = jnp.where(
            row % 2 == 0,
            jnp.concatenate([solved[1:], solved[:1]], axis=0),
            jnp.concatenate([solved[7:], solved[:7]], axis=0),
        )
        solved = same * solved + beside * partner
        pieces = [wide(solved[j : j + 1]) for j in range(8)]
        for q in range(p + 1, panels):
            terms = [wide(left[q][:, at + j : at + j + 1]) * pieces[j] for j in range(8)]
            left[q] = jnp.where(here, 0.0, left[q]) - tree_sum(terms)


def inverse_factor(gram):
    return pl.pallas_call(
        inverse_kernel,
        out_shape=jax.ShapeDtypeStruct((RANK, RANK), f32),
        compiler_params=pltpu.CompilerParams(vmem_limit_bytes=16 * MIB),
        cost_estimate=pl.CostEstimate(flops=3 * 10**9, bytes_accessed=10**5, transcendentals=0),
        name="inverse_factor",
    )(gram)


def basis_kernel(core, left_mean, own, other, basis, operand, token):
    token[...] = jnp.zeros(token.shape, f32)
    for i, inverse in ((core[0], own), (1 - core[0], other)):
        rows = dot_wide(left_mean[:, i].reshape(ROWS, RANK), inverse[...].T)
        basis[i] = rows
        operand[i] = stacked(rows * (1.0 / math.sqrt(FEATURES)))


def basis_rows(core, left_mean, own, other):
    return pl.pallas_call(
        basis_kernel,
        in_specs=[pl.BlockSpec(memory_space=pltpu.SMEM)] + [pl.BlockSpec(memory_space=pltpu.VMEM)] * 3,
        out_shape=[
            jax.ShapeDtypeStruct((MATRICES, ROWS, RANK), f32),
            jax.ShapeDtypeStruct((MATRICES, ROWS, 2 * RANK), bf16),
            jax.ShapeDtypeStruct((8, RANK), f32),
        ],
        compiler_params=pltpu.CompilerParams(vmem_limit_bytes=16 * MIB),
        cost_estimate=pl.CostEstimate(flops=8 * 10**8, bytes_accessed=2 * 10**6, transcendentals=0),
        name="basis_rows",
    )(core, left_mean, own, other)


def factor_kernel(*refs):
    *parts, inverse, out = refs
    total = tree_sum([part[...] for part in parts])
    rows = dot_wide(total, inverse[...].T) * (1.0 / (32 * math.sqrt(FEATURES)))
    for i in range(out.shape[0]):
        out[i] = rows


def factor_rows(parts, inverse, copies):
    return pl.pallas_call(
        factor_kernel,
        out_shape=jax.ShapeDtypeStruct((copies,) + parts[0].shape, f32),
        compiler_params=pltpu.CompilerParams(vmem_limit_bytes=16 * MIB),
        cost_estimate=pl.CostEstimate(flops=10**8, bytes_accessed=4 * 10**5, transcendentals=0),
        name="factor_rows",
    )(*parts, inverse)


def tie_kernel(x, after, out):
    del x, after, out


def tie(x, after):
    return pl.pallas_call(
        tie_kernel,
        in_specs=[pl.BlockSpec(memory_space=pl.ANY), pl.BlockSpec(memory_space=pltpu.VMEM)],
        out_specs=pl.BlockSpec(memory_space=pl.ANY),
        out_shape=pltpu.VMEM(x.shape, x.dtype),
        input_output_aliases={0: 0},
        compiler_params=pltpu.CompilerParams(vmem_limit_bytes=MIB),
        name="tie",
    )(in_vmem(x), after)


def fetches(which, gradient, feedback, gradient_in, feedback_in, sems, i):
    rows = gradient_in.shape[1]
    at = pl.ds(i * rows, rows)
    return (
        pltpu.make_async_copy(gradient.at[which, at], gradient_in.at[i], sems.at[0, i]),
        pltpu.make_async_copy(feedback.at[which, at], feedback_in.at[i], sems.at[1, i]),
    )


def merge_arrived(which, gradient, feedback, gradient_in, feedback_in, sems, merged):
    steps, rows, _ = gradient_in.shape
    for i in range(steps):
        for copy in fetches(which, gradient, feedback, gradient_in, feedback_in, sems, i):
            copy.wait()
        merged[i * rows : (i + 1) * rows] = gradient_in[i].astype(f32) + feedback_in[i]


def fetch_scratch(steps):
    rows = ROWS // steps
    return [
        pltpu.VMEM((steps, rows, WIDTH), bf16),
        pltpu.VMEM((steps, rows, WIDTH), f32),
        pltpu.SemaphoreType.DMA((2, steps)),
    ]


def merge_kernel(which, gradient, feedback, after, merged, token, *scratch):
    del after
    token[...] = jnp.zeros(token.shape, f32)
    arrays = (which[0], gradient, feedback, *scratch)
    for i in range(scratch[0].shape[0]):
        for copy in fetches(*arrays, i):
            copy.start()
    merge_arrived(*arrays, merged)


def merge(which, gradient, feedback, after):
    return pl.pallas_call(
        merge_kernel,
        in_specs=[pl.BlockSpec(memory_space=pltpu.SMEM)]
        + [pl.BlockSpec(memory_space=pltpu.HBM)] * 2
        + [pl.BlockSpec(memory_space=pltpu.VMEM)],
        out_shape=[jax.ShapeDtypeStruct((ROWS, WIDTH), f32), jax.ShapeDtypeStruct((8, RANK), f32)],
        scratch_shapes=fetch_scratch(2),
        compiler_params=pltpu.CompilerParams(vmem_limit_bytes=16 * MIB),
        cost_estimate=pl.CostEstimate(flops=10**8, bytes_accessed=5 * 10**6, transcendentals=0),
        name="merge",
    )(which, gradient, feedback, after)


def finish_kernel(which, merged, operand, right, *rest):
    *rest, renewed_out, turned, sems = rest
    w = which[0]
    steps, rows, _ = renewed_out.shape
    if len(rest) > 4:
        gradient, feedback, renewed, factor, merged_next, *scratch = rest
        arrays = (1 - w, gradient, feedback, *scratch)
        for i in range(scratch[0].shape[0]):
            for copy in fetches(*arrays, i):
                copy.start()
    else:
        renewed, factor = rest[-2:]

    def store(i):
        return pltpu.make_async_copy(renewed_out.at[i], renewed.at[w, pl.ds(i * rows, rows)], sems.at[i])

    store_factor = pltpu.make_async_copy(right, factor.at[w], sems.at[steps])
    store_factor.start()
    high, low = halves(right[...])
    turned[:, :RANK] = high
    turned[:, RANK : 2 * RANK] = high
    turned[:, 2 * RANK :] = low
    for i in range(steps):
        at = slice(i * rows, (i + 1) * rows)
        both = operand[w, at]
        approx = dot(both, turned[:, : 2 * RANK], NT) + dot(both[:, :RANK], turned[:, 2 * RANK :], NT)
        renewed_out[i] = merged[at] - approx
        store(i).start()
    if len(rest) > 4:
        merge_arrived(*arrays, merged_next)
    for i in range(steps):
        store(i).wait()
    store_factor.wait()


def finish(which, merged, operand, right, ahead=(), before=(), steps=2):
    rows = ROWS // steps
    outs = [
        jax.ShapeDtypeStruct((MATRICES, ROWS, WIDTH), f32),
        jax.ShapeDtypeStruct((MATRICES, WIDTH, RANK), f32),
    ]
    return pl.pallas_call(
        finish_kernel,
        in_specs=[pl.BlockSpec(memory_space=pltpu.SMEM)]
        + [pl.BlockSpec(memory_space=pltpu.VMEM)] * 3
        + [pl.BlockSpec(memory_space=pltpu.HBM)] * len(ahead)
        + [pl.BlockSpec(memory_space=pl.ANY)] * len(before),
        out_specs=[pl.BlockSpec(memory_space=pl.ANY)] * 2 + [pl.BlockSpec(memory_space=pltpu.VMEM)] * bool(ahead),
        out_shape=outs + [jax.ShapeDtypeStruct((ROWS, WIDTH), f32)] * bool(ahead),
        scratch_shapes=fetch_scratch(2) * bool(ahead)
        + [
            pltpu.VMEM((steps, rows, WIDTH), f32),
            pltpu.VMEM((WIDTH, 3 * RANK), bf16),
            pltpu.SemaphoreType.DMA((steps + 1,)),
        ],
        input_output_aliases={4: 0, 5: 1} if before else {},
        compiler_params=pltpu.CompilerParams(vmem_limit_bytes=24 * MIB),
        cost_estimate=pl.CostEstimate(flops=8 * 10**8, bytes_accessed=6 * 10**6, transcendentals=0),
        name="finish",
    )(which, merged, operand, right, *ahead, *before)


def share_kernel(*refs, scale, count):
    parts, out = refs[:count], refs[-1]
    if count == 1:
        parts = [parts[0][i] for i in range(parts[0].shape[0])]
    else:
        parts = [part[0] for part in parts]
    total = tree_sum(parts) * scale
    for i in range(out.shape[0]):
        out[i] = total


def share(parts, copies, scale, after=()):
    parts = parts if isinstance(parts, list) else [parts]
    return pl.pallas_call(
        functools.partial(share_kernel, scale=scale, count=len(parts)),
        out_shape=jax.ShapeDtypeStruct((copies,) + parts[0].shape[1:], f32),
        compiler_params=pltpu.CompilerParams(vmem_limit_bytes=8 * MIB),
        name="share",
    )(*parts, *after)


def parcel_kernel(place, right, gram, arrived, out, gram_sum):
    gram_sum[...] = gram[...] + arrived[WIDTH:]
    piece = gram_sum[pl.ds(pl.multiple_of(place[0] * PIECE, PIECE), PIECE)]
    for i in range(BOX):
        at = slice(i * SHARE, (i + 1) * SHARE)
        out[i, :SHARE] = right[at] + arrived[at]
        out[i, SHARE:] = piece


def parcels(place, right, gram, arrived):
    return pl.pallas_call(
        parcel_kernel,
        in_specs=[pl.BlockSpec(memory_space=pltpu.SMEM)] + [pl.BlockSpec(memory_space=pltpu.VMEM)] * 3,
        out_shape=jax.ShapeDtypeStruct((BOX, SHARE + PIECE, RANK), f32),
        scratch_shapes=[pltpu.VMEM((RANK, RANK), f32)],
        compiler_params=pltpu.CompilerParams(vmem_limit_bytes=8 * MIB),
        name="parcels",
    )(place, right, gram, arrived)


def unpack_kernel(parts, total, gram):
    total[...] = tree_sum([parts[i, :SHARE] for i in range(BOX)])
    for k in range(RANK // PIECE):
        gram[k * PIECE : (k + 1) * PIECE] = tree_sum([parts[8 * x + k, SHARE:] for x in range(4)])


def unpack(parts):
    return pl.pallas_call(
        unpack_kernel,
        out_shape=[jax.ShapeDtypeStruct((SHARE, RANK), f32), jax.ShapeDtypeStruct((RANK, RANK), f32)],
        compiler_params=pltpu.CompilerParams(vmem_limit_bytes=8 * MIB),
        name="unpack",
    )(parts)


def exchange(x, axes):
    return lax.all_to_all(x, axes, 0, 0, tiled=True)


def swap(x):
    return lax.ppermute(x, "core", [(0, 1), (1, 0)])


def rounds(x, axis):
    return [x] + [lax.ppermute(x, axis, [(i, i ^ s) for i in range(4)]) for s in (1, 3, 2)]


def shards(gradient, feedback, right_prior):
    own = lax.axis_index("core")[None]
    other = 1 - own
    place = lax.axis_index(('zl', 'y'))[None]
    column, box = ('zl', 'y'), ('x', 'zl', 'y')
    gradient, feedback, right_prior = in_hbm(gradient[0]), in_hbm(feedback[0]), in_hbm(right_prior)
    left, merged = left_terms(other, place, gradient, feedback, right_prior)
    left = rounds(share(exchange(left, column), 1, 1.0 / 32), "zh")
    left_mean = exchange(share(left, 8, 1.0), column)

    right_other, gram = right_terms(other, merged, left_mean, True)
    arrived = swap(right_other)
    right = right_terms(own, merged, left_mean, False)[0]
    parts = exchange(parcels(place, right, gram, arrived), box)
    total, gram = unpack(parts)
    totals = rounds(total, "zh")
    inverse = inverse_factor(gram)
    right = exchange(factor_rows(totals, inverse, 32), box).reshape(WIDTH, RANK)
    basis, operand, token = basis_rows(own, left_mean, inverse, swap(inverse))
    merged, token = merge(own, gradient, feedback, token)
    right = tie(right, token)

    *done, merged = finish(own, merged, operand, right, (gradient, feedback))
    renewed, factor = finish(other, merged, operand, swap(right), (), tuple(done))
    return renewed[None], basis, factor


def solution(mesh):
    chips = Mesh(mesh.devices.reshape(4, 2, 4, 4, 2), ("zh", "zl", "y", "x", "core"))
    rep, fsdp = ("zh", "zl", "y"), ("x", "core")
    in_specs = (P(rep, None, fsdp, None), P(rep, None, fsdp, None), P())
    out_specs = (P(rep, None, fsdp, None), P(None, fsdp, None), P())
    return jax.shard_map(shards, mesh=chips, in_specs=in_specs, out_specs=out_specs, check_vma=False)
```

```python
import functools
import math

import jax
import jax.numpy as jnp
from jax import lax
from jax.experimental import pallas as pl
from jax.experimental.pallas import tpu as pltpu
from jax.sharding import Mesh, PartitionSpec as P

FEATURES = 4096
WIDTH = 1024
RANK = 128
MATRICES = 2
ROWS = 512
CHUNK = 64
BOX = 32
SHARE = WIDTH // BOX
PIECE = 16
ridge_relative = 0.001
ridge_absolute = 1e-06
MIB = 1 << 20
f32 = jnp.float32
bf16 = jnp.bfloat16


def halves(x):
    high = x.astype(bf16)
    return high, (x - high.astype(f32)).astype(bf16)


def dot(a, b, dims):
    return lax.dot_general(a, b, (dims, ((), ())), preferred_element_type=f32)


def in_vmem(x):
    return pltpu.with_memory_space_constraint(x, pltpu.VMEM)


def in_hbm(x):
    return pltpu.with_memory_space_constraint(x, pltpu.HBM)


NN = ((1,), (0,))
NT = ((1,), (1,))
TN = ((0,), (0,))


def dot_wide(a, b):
    a_high, a_low = halves(a)
    b_high, b_low = halves(b)
    both = dot(a_high, jnp.concatenate([b_high, b_low], axis=1), NN)
    return both[:, :RANK] + (both[:, RANK:] + dot(a_low, b_high, NN))


def dot_deep(a, b):
    a_high, a_low = halves(a)
    b_high, b_low = halves(b)
    both = jnp.concatenate([a_high, a_low], axis=1)
    return dot(both, jnp.concatenate([b_high, b_high], axis=1), NT) + dot(a_high, b_low, NT)


def left_kernel(other, place, gradient, feedback, prior, left, merged, gradient_in, feedback_in, prior_in, sems, prior_sem):
    del other, place
    steps = gradient_in.shape[0]
    rows = ROWS * MATRICES // steps
    per = steps // MATRICES

    def fetch(i):
        m, at = i // per, i % per * rows
        return (
            pltpu.make_async_copy(gradient.at[m, pl.ds(at, rows)], gradient_in.at[i], sems.at[0, i]),
            pltpu.make_async_copy(feedback.at[m, pl.ds(at, rows)], feedback_in.at[i], sems.at[1, i]),
        )

    def fetch_prior(m):
        return pltpu.make_async_copy(prior.at[m], prior_in.at[m], prior_sem.at[m])

    for i in range(steps):
        if i % per == 0:
            fetch_prior(i // per).start()
        for copy in fetch(i):
            copy.start()
    for i in range(steps):
        m, at = i // per, i % per * rows
        if at == 0:
            fetch_prior(m).wait()
        for copy in fetch(i):
            copy.wait()
        total = gradient_in[i].astype(f32) + feedback_in[i]
        merged[m, at : at + rows] = total
        left[at // CHUNK : (at + rows) // CHUNK, m] = dot_wide(total, prior_in[m]).reshape(rows // CHUNK, CHUNK, RANK)


def left_terms(other, place, gradient, feedback, right_prior, steps=2):
    rows = ROWS * MATRICES // steps
    return pl.pallas_call(
        left_kernel,
        in_specs=[pl.BlockSpec(memory_space=pltpu.SMEM)] * 2 + [pl.BlockSpec(memory_space=pltpu.HBM)] * 3,
        out_specs=[pl.BlockSpec(memory_space=pltpu.VMEM)] * 2,
        out_shape=[
            jax.ShapeDtypeStruct((ROWS // CHUNK, MATRICES, CHUNK, RANK), f32),
            jax.ShapeDtypeStruct((MATRICES, ROWS, WIDTH), f32),
        ],
        scratch_shapes=[
            pltpu.VMEM((steps, rows, WIDTH), bf16),
            pltpu.VMEM((steps, rows, WIDTH), f32),
            pltpu.VMEM((MATRICES, WIDTH, RANK), f32),
            pltpu.SemaphoreType.DMA((2, steps)),
            pltpu.SemaphoreType.DMA((MATRICES,)),
        ],
        compiler_params=pltpu.CompilerParams(vmem_limit_bytes=24 * MIB),
        name="left_terms",
    )(other, place, gradient, feedback, right_prior)


def stacked(left):
    return jnp.concatenate(halves(left), axis=1)


def gram_of(both):
    square = dot(both, both, TN)
    return square[:RANK, :RANK] + (square[RANK:, :RANK] + square[:RANK, RANK:] + square[RANK:, RANK:])


def right_kernel(which, merged, left_mean, right, *gram):
    i = which[0]
    both = stacked(left_mean[:, i].reshape(ROWS, RANK))
    if gram:
        right[WIDTH:] = gram_of(both)
        gram[0][...] = gram_of(stacked(left_mean[:, 1 - i].reshape(ROWS, RANK)))
    cols = WIDTH // 2
    for at in range(0, WIDTH, cols):
        merged_high, merged_low = halves(merged[i, :, at : at + cols])
        double = dot(both, merged_high, TN)
        total = double[:RANK] + (double[RANK:] + dot(both[:, :RANK], merged_low, TN))
        right[at : at + cols] = total.T


def right_terms(which, merged, left_mean, with_gram):
    return pl.pallas_call(
        right_kernel,
        in_specs=[pl.BlockSpec(memory_space=pltpu.SMEM)] + [pl.BlockSpec(memory_space=pltpu.VMEM)] * 2,
        out_shape=[jax.ShapeDtypeStruct((WIDTH + RANK * with_gram, RANK), f32)]
        + [jax.ShapeDtypeStruct((RANK, RANK), f32)] * with_gram,
        compiler_params=pltpu.CompilerParams(vmem_limit_bytes=24 * MIB),
        cost_estimate=pl.CostEstimate(flops=8 * 10**8, bytes_accessed=4 * 10**6, transcendentals=0),
        name="right_terms",
    )(which, merged, left_mean)


def tree_sum(terms):
    while len(terms) > 1:
        terms = [a + b for a, b in zip(terms[::2], terms[1::2])]
    return terms[0]


def inverse_kernel(gram, out):
    rows = lax.broadcasted_iota(jnp.int32, (RANK, RANK), 0)
    cols = lax.broadcasted_iota(jnp.int32, (RANK, RANK), 1)
    diagonal = rows == cols
    matrix = gram[...] * (1.0 / FEATURES)
    trace = jnp.sum(jnp.where(diagonal, matrix, 0.0))
    ridge = ridge_relative * (trace / RANK) + ridge_absolute
    matrix = jnp.where(diagonal, matrix + ridge, matrix)
    panels = RANK // 8
    left = [matrix[8 * q : 8 * q + 8] for q in range(panels)]
    row = lax.broadcasted_iota(jnp.int32, (8, RANK), 0)
    lane = lax.broadcasted_iota(jnp.int32, (8, RANK), 1)

    def wide(x):
        return jnp.broadcast_to(x, (8, RANK))

    for p in range(panels):
        at = 8 * p
        here = (lane >= at) & (lane < at + 8)
        col = [wide(left[p][:, at + j : at + j + 1]) for j in range(8)]
        solved = reduced = jnp.where(here, jnp.where(lane - at == row, 1.0, 0.0), left[p])
        pivots = same = beside = jnp.ones((8, RANK), f32)
        for j in range(0, 8, 2):
            a, b, d = wide(col[j][j : j + 1]), wide(col[j + 1][j : j + 1]), wide(col[j + 1][j + 1 : j + 2])
            det = a * d - b * b
            scale = 1.0 / det
            first, second = row == j, row == j + 1
            away = (row < j) | (row > j + 1)
            factor_0 = jnp.where(away, col[j] * d - col[j + 1] * b, 0.0) * scale
            factor_1 = jnp.where(away, col[j + 1] * a - col[j] * b, 0.0) * scale
            for t in range(j + 2, 8):
                col[t] = col[t] - (factor_0 * wide(col[t][j : j + 1]) + factor_1 * wide(col[t][j + 1 : j + 2]))
            row_0, row_1 = wide(reduced[j : j + 1]), wide(reduced[j + 1 : j + 2])
            scale_a = 1.0 / a
            change = factor_0 * row_0 + factor_1 * row_1
            solved = solved - change
            reduced = reduced - jnp.where(row > j + 1, change, jnp.where(second, (b * scale_a) * row_0, 0.0))
            pivots = jnp.where(first, a, jnp.where(second, det * scale_a, pivots))
            same = jnp.where(first, d * scale, jnp.where(second, a * scale, same))
            beside = jnp.where(first | second, -(b * scale), beside)
        out[at : at + 8] = jnp.where(lane < at + 8, reduced * lax.rsqrt(pivots), 0.0)
        if p + 1 == panels:
            break
        partner = jnp.where(
            row % 2 == 0,
            jnp.concatenate([solved[1:], solved[:1]], axis=0),
            jnp.concatenate([solved[7:], solved[:7]], axis=0),
        )
        solved = same * solved + beside * partner
        pieces = [wide(solved[j : j + 1]) for j in range(8)]
        for q in range(p + 1, panels):
            terms = [wide(left[q][:, at + j : at + j + 1]) * pieces[j] for j in range(8)]
            left[q] = jnp.where(here, 0.0, left[q]) - tree_sum(terms)


def inverse_factor(gram):
    return pl.pallas_call(
        inverse_kernel,
        out_shape=jax.ShapeDtypeStruct((RANK, RANK), f32),
        compiler_params=pltpu.CompilerParams(vmem_limit_bytes=16 * MIB),
        cost_estimate=pl.CostEstimate(flops=3 * 10**9, bytes_accessed=10**5, transcendentals=0),
        name="inverse_factor",
    )(gram)


def factor_kernel(*refs):
    *parts, inverse, out = refs
    total = tree_sum([part[...] for part in parts])
    rows = dot_wide(total, inverse[...].T) * (1.0 / (32 * math.sqrt(FEATURES)))
    for i in range(out.shape[0]):
        out[i] = rows


def factor_rows(parts, inverse, copies):
    return pl.pallas_call(
        factor_kernel,
        out_shape=jax.ShapeDtypeStruct((copies,) + parts[0].shape, f32),
        compiler_params=pltpu.CompilerParams(vmem_limit_bytes=16 * MIB),
        cost_estimate=pl.CostEstimate(flops=10**8, bytes_accessed=4 * 10**5, transcendentals=0),
        name="factor_rows",
    )(*parts, inverse)


def tie_kernel(x, after, out):
    del x, after, out


def tie(x, after):
    return pl.pallas_call(
        tie_kernel,
        in_specs=[pl.BlockSpec(memory_space=pl.ANY), pl.BlockSpec(memory_space=pltpu.VMEM)],
        out_specs=pl.BlockSpec(memory_space=pl.ANY),
        out_shape=pltpu.VMEM(x.shape, x.dtype),
        input_output_aliases={0: 0},
        compiler_params=pltpu.CompilerParams(vmem_limit_bytes=MIB),
        name="tie",
    )(in_vmem(x), after)


def finish_kernel(which, merged, left_mean, inverse, right, *rest):
    renewed, basis, factor, renewed_out, basis_out, turned, sems = rest[-7:]
    w = which[0]
    steps, rows, _ = renewed_out.shape

    def store(i):
        return pltpu.make_async_copy(renewed_out.at[i], renewed.at[w, pl.ds(i * rows, rows)], sems.at[i])

    store_factor = pltpu.make_async_copy(right, factor.at[w], sems.at[steps])
    store_basis = pltpu.make_async_copy(basis_out, basis.at[w], sems.at[steps + 1])
    store_factor.start()
    left_basis = dot_wide(left_mean[:, w].reshape(ROWS, RANK), inverse[...].T)
    basis_out[...] = left_basis
    store_basis.start()
    operand = stacked(left_basis * (1.0 / math.sqrt(FEATURES)))
    high, low = halves(right[...])
    turned[:, :RANK] = high
    turned[:, RANK : 2 * RANK] = high
    turned[:, 2 * RANK :] = low
    for i in range(steps):
        at = slice(i * rows, (i + 1) * rows)
        both = operand[at]
        approx = dot(both, turned[:, : 2 * RANK], NT) + dot(both[:, :RANK], turned[:, 2 * RANK :], NT)
        renewed_out[i] = merged[w, at] - approx
        store(i).start()
    store_factor.wait()
    store_basis.wait()
    for i in range(steps):
        store(i).wait()


def finish(which, merged, left_mean, inverse, right, before=(), steps=2):
    rows = ROWS // steps
    return pl.pallas_call(
        finish_kernel,
        in_specs=[pl.BlockSpec(memory_space=pltpu.SMEM)]
        + [pl.BlockSpec(memory_space=pltpu.VMEM)] * 4
        + [pl.BlockSpec(memory_space=pl.ANY)] * len(before),
        out_specs=[pl.BlockSpec(memory_space=pl.ANY)] * 3,
        out_shape=[
            jax.ShapeDtypeStruct((MATRICES, ROWS, WIDTH), f32),
            jax.ShapeDtypeStruct((MATRICES, ROWS, RANK), f32),
            jax.ShapeDtypeStruct((MATRICES, WIDTH, RANK), f32),
        ],
        scratch_shapes=[
            pltpu.VMEM((steps, rows, WIDTH), f32),
            pltpu.VMEM((ROWS, RANK), f32),
            pltpu.VMEM((WIDTH, 3 * RANK), bf16),
            pltpu.SemaphoreType.DMA((steps + 2,)),
        ],
        input_output_aliases={5: 0, 6: 1, 7: 2} if before else {},
        compiler_params=pltpu.CompilerParams(vmem_limit_bytes=24 * MIB),
        cost_estimate=pl.CostEstimate(flops=8 * 10**8, bytes_accessed=6 * 10**6, transcendentals=0),
        name="finish",
    )(which, merged, left_mean, inverse, right, *before)


def share_kernel(*refs, scale, count):
    parts, out = refs[:count], refs[-1]
    if count == 1:
        parts = [parts[0][i] for i in range(parts[0].shape[0])]
    else:
        parts = [part[0] for part in parts]
    total = tree_sum(parts) * scale
    for i in range(out.shape[0]):
        out[i] = total


def share(parts, copies, scale, after=()):
    parts = parts if isinstance(parts, list) else [parts]
    return pl.pallas_call(
        functools.partial(share_kernel, scale=scale, count=len(parts)),
        out_shape=jax.ShapeDtypeStruct((copies,) + parts[0].shape[1:], f32),
        compiler_params=pltpu.CompilerParams(vmem_limit_bytes=8 * MIB),
        name="share",
    )(*parts, *after)


def parcel_kernel(place, right, gram, arrived, out, gram_sum):
    gram_sum[...] = gram[...] + arrived[WIDTH:]
    piece = gram_sum[pl.ds(pl.multiple_of(place[0] * PIECE, PIECE), PIECE)]
    for i in range(BOX):
        at = slice(i * SHARE, (i + 1) * SHARE)
        out[i, :SHARE] = right[at] + arrived[at]
        out[i, SHARE:] = piece


def parcels(place, right, gram, arrived):
    return pl.pallas_call(
        parcel_kernel,
        in_specs=[pl.BlockSpec(memory_space=pltpu.SMEM)] + [pl.BlockSpec(memory_space=pltpu.VMEM)] * 3,
        out_shape=jax.ShapeDtypeStruct((BOX, SHARE + PIECE, RANK), f32),
        scratch_shapes=[pltpu.VMEM((RANK, RANK), f32)],
        compiler_params=pltpu.CompilerParams(vmem_limit_bytes=8 * MIB),
        name="parcels",
    )(place, right, gram, arrived)


def unpack_kernel(parts, total, gram):
    total[...] = tree_sum([parts[i, :SHARE] for i in range(BOX)])
    for k in range(RANK // PIECE):
        gram[k * PIECE : (k + 1) * PIECE] = tree_sum([parts[8 * x + k, SHARE:] for x in range(4)])


def unpack(parts):
    return pl.pallas_call(
        unpack_kernel,
        out_shape=[jax.ShapeDtypeStruct((SHARE, RANK), f32), jax.ShapeDtypeStruct((RANK, RANK), f32)],
        compiler_params=pltpu.CompilerParams(vmem_limit_bytes=8 * MIB),
        name="unpack",
    )(parts)


def exchange(x, axes):
    return lax.all_to_all(x, axes, 0, 0, tiled=True)


def swap(x):
    return lax.ppermute(x, "core", [(0, 1), (1, 0)])


def rounds(x, axis):
    return [x] + [lax.ppermute(x, axis, [(i, i ^ s) for i in range(4)]) for s in (1, 3, 2)]


def shards(gradient, feedback, right_prior):
    own = lax.axis_index("core")[None]
    other = 1 - own
    place = lax.axis_index(('zl', 'y'))[None]
    column, box = ('zl', 'y'), ('x', 'zl', 'y')
    gradient, feedback, right_prior = in_hbm(gradient[0]), in_hbm(feedback[0]), in_hbm(right_prior)
    left, merged = left_terms(other, place, gradient, feedback, right_prior)
    left = rounds(share(exchange(left, column), 1, 1.0 / 32), "zh")
    left_mean = exchange(share(left, 8, 1.0), column)

    right_other, gram = right_terms(other, merged, left_mean, True)
    arrived = swap(right_other)
    right = right_terms(own, merged, left_mean, False)[0]
    parts = exchange(parcels(place, right, gram, arrived), box)
    total, gram = unpack(parts)
    totals = rounds(total, "zh")
    inverse = inverse_factor(gram)
    right = exchange(factor_rows(totals, inverse, 32), box).reshape(WIDTH, RANK)
    inverse = tie(inverse, right)
    arrived = swap(inverse), swap(right)
    done = finish(own, merged, left_mean, inverse, right)
    renewed, basis, factor = finish(other, merged, left_mean, *arrived, tuple(done))
    return renewed[None], basis, factor


def solution(mesh):
    chips = Mesh(mesh.devices.reshape(4, 2, 4, 4, 2), ("zh", "zl", "y", "x", "core"))
    rep, fsdp = ("zh", "zl", "y"), ("x", "core")
    in_specs = (P(rep, None, fsdp, None), P(rep, None, fsdp, None), P())
    out_specs = (P(rep, None, fsdp, None), P(None, fsdp, None), P())
    return jax.shard_map(shards, mesh=chips, in_specs=in_specs, out_specs=out_specs, check_vma=False)
```

```python
import functools
import math

import jax
import jax.numpy as jnp
from jax import lax
from jax.experimental import pallas as pl
from jax.experimental.pallas import tpu as pltpu
from jax.sharding import Mesh, PartitionSpec as P

FEATURES = 4096
WIDTH = 1024
RANK = 128
MATRICES = 2
ROWS = 512
CHUNK = 64
BOX = 32
SHARE = WIDTH // BOX
PIECE = 16
ridge_relative = 0.001
ridge_absolute = 1e-06
MIB = 1 << 20
f32 = jnp.float32
bf16 = jnp.bfloat16


def halves(x):
    high = x.astype(bf16)
    return high, (x - high.astype(f32)).astype(bf16)


def dot(a, b, dims):
    return lax.dot_general(a, b, (dims, ((), ())), preferred_element_type=f32)


def in_vmem(x):
    return pltpu.with_memory_space_constraint(x, pltpu.VMEM)


def in_hbm(x):
    return pltpu.with_memory_space_constraint(x, pltpu.HBM)


NN = ((1,), (0,))
NT = ((1,), (1,))
TN = ((0,), (0,))


def dot_wide(a, b):
    a_high, a_low = halves(a)
    b_high, b_low = halves(b)
    both = dot(a_high, jnp.concatenate([b_high, b_low], axis=1), NN)
    return both[:, :RANK] + (both[:, RANK:] + dot(a_low, b_high, NN))


def dot_deep(a, b):
    a_high, a_low = halves(a)
    b_high, b_low = halves(b)
    both = jnp.concatenate([a_high, a_low], axis=1)
    return dot(both, jnp.concatenate([b_high, b_high], axis=1), NT) + dot(a_high, b_low, NT)


def left_kernel(other, place, gradient, feedback, prior, left, merged, gradient_in, feedback_in, prior_in, sems, prior_sem):
    del other, place
    steps = gradient_in.shape[0]
    rows = ROWS * MATRICES // steps
    per = steps // MATRICES

    def fetch(i):
        m, at = i // per, i % per * rows
        return (
            pltpu.make_async_copy(gradient.at[m, pl.ds(at, rows)], gradient_in.at[i], sems.at[0, i]),
            pltpu.make_async_copy(feedback.at[m, pl.ds(at, rows)], feedback_in.at[i], sems.at[1, i]),
        )

    def fetch_prior(m):
        return pltpu.make_async_copy(prior.at[m], prior_in.at[m], prior_sem.at[m])

    for i in range(steps):
        if i % per == 0:
            fetch_prior(i // per).start()
        for copy in fetch(i):
            copy.start()
    for i in range(steps):
        m, at = i // per, i % per * rows
        if at == 0:
            fetch_prior(m).wait()
        for copy in fetch(i):
            copy.wait()
        total = gradient_in[i].astype(f32) + feedback_in[i]
        merged[m, at : at + rows] = total
        left[at // CHUNK : (at + rows) // CHUNK, m] = dot_wide(total, prior_in[m]).reshape(rows // CHUNK, CHUNK, RANK)


def left_terms(other, place, gradient, feedback, right_prior, steps=2):
    rows = ROWS * MATRICES // steps
    return pl.pallas_call(
        left_kernel,
        in_specs=[pl.BlockSpec(memory_space=pltpu.SMEM)] * 2 + [pl.BlockSpec(memory_space=pltpu.HBM)] * 3,
        out_specs=[pl.BlockSpec(memory_space=pltpu.VMEM)] * 2,
        out_shape=[
            jax.ShapeDtypeStruct((ROWS // CHUNK, MATRICES, CHUNK, RANK), f32),
            jax.ShapeDtypeStruct((MATRICES, ROWS, WIDTH), f32),
        ],
        scratch_shapes=[
            pltpu.VMEM((steps, rows, WIDTH), bf16),
            pltpu.VMEM((steps, rows, WIDTH), f32),
            pltpu.VMEM((MATRICES, WIDTH, RANK), f32),
            pltpu.SemaphoreType.DMA((2, steps)),
            pltpu.SemaphoreType.DMA((MATRICES,)),
        ],
        compiler_params=pltpu.CompilerParams(vmem_limit_bytes=24 * MIB),
        name="left_terms",
    )(other, place, gradient, feedback, right_prior)


def stacked(left):
    return jnp.concatenate(halves(left), axis=1)


def gram_of(both):
    square = dot(both, both, TN)
    return square[:RANK, :RANK] + (square[RANK:, :RANK] + square[:RANK, RANK:] + square[RANK:, RANK:])


def right_kernel(which, merged, left_mean, right, *gram):
    i = which[0]
    both = stacked(left_mean[:, i].reshape(ROWS, RANK))
    if gram:
        right[WIDTH:] = gram_of(both)
        gram[0][...] = gram_of(stacked(left_mean[:, 1 - i].reshape(ROWS, RANK)))
    cols = WIDTH // 2
    for at in range(0, WIDTH, cols):
        merged_high, merged_low = halves(merged[i, :, at : at + cols])
        double = dot(both, merged_high, TN)
        total = double[:RANK] + (double[RANK:] + dot(both[:, :RANK], merged_low, TN))
        right[at : at + cols] = total.T


def right_terms(which, merged, left_mean, with_gram):
    return pl.pallas_call(
        right_kernel,
        in_specs=[pl.BlockSpec(memory_space=pltpu.SMEM)] + [pl.BlockSpec(memory_space=pltpu.VMEM)] * 2,
        out_shape=[jax.ShapeDtypeStruct((WIDTH + RANK * with_gram, RANK), f32)]
        + [jax.ShapeDtypeStruct((RANK, RANK), f32)] * with_gram,
        compiler_params=pltpu.CompilerParams(vmem_limit_bytes=24 * MIB),
        cost_estimate=pl.CostEstimate(flops=8 * 10**8, bytes_accessed=4 * 10**6, transcendentals=0),
        name="right_terms",
    )(which, merged, left_mean)


def tree_sum(terms):
    while len(terms) > 1:
        terms = [a + b for a, b in zip(terms[::2], terms[1::2])]
    return terms[0]


def inverse_kernel(gram, out):
    rows = lax.broadcasted_iota(jnp.int32, (RANK, RANK), 0)
    cols = lax.broadcasted_iota(jnp.int32, (RANK, RANK), 1)
    diagonal = rows == cols
    matrix = gram[...] * (1.0 / FEATURES)
    trace = jnp.sum(jnp.where(diagonal, matrix, 0.0))
    ridge = ridge_relative * (trace / RANK) + ridge_absolute
    matrix = jnp.where(diagonal, matrix + ridge, matrix)
    panels = RANK // 8
    left = [matrix[8 * q : 8 * q + 8] for q in range(panels)]
    row = lax.broadcasted_iota(jnp.int32, (8, RANK), 0)
    lane = lax.broadcasted_iota(jnp.int32, (8, RANK), 1)

    def wide(x):
        return jnp.broadcast_to(x, (8, RANK))

    for p in range(panels):
        at = 8 * p
        here = (lane >= at) & (lane < at + 8)
        col = [wide(left[p][:, at + j : at + j + 1]) for j in range(8)]
        solved = reduced = jnp.where(here, jnp.where(lane - at == row, 1.0, 0.0), left[p])
        pivots = same = beside = jnp.ones((8, RANK), f32)
        for j in range(0, 8, 2):
            a, b, d = wide(col[j][j : j + 1]), wide(col[j + 1][j : j + 1]), wide(col[j + 1][j + 1 : j + 2])
            det = a * d - b * b
            scale = 1.0 / det
            first, second = row == j, row == j + 1
            away = (row < j) | (row > j + 1)
            factor_0 = jnp.where(away, col[j] * d - col[j + 1] * b, 0.0) * scale
            factor_1 = jnp.where(away, col[j + 1] * a - col[j] * b, 0.0) * scale
            for t in range(j + 2, 8):
                col[t] = col[t] - (factor_0 * wide(col[t][j : j + 1]) + factor_1 * wide(col[t][j + 1 : j + 2]))
            row_0, row_1 = wide(reduced[j : j + 1]), wide(reduced[j + 1 : j + 2])
            scale_a = 1.0 / a
            change = factor_0 * row_0 + factor_1 * row_1
            solved = solved - change
            reduced = reduced - jnp.where(row > j + 1, change, jnp.where(second, (b * scale_a) * row_0, 0.0))
            pivots = jnp.where(first, a, jnp.where(second, det * scale_a, pivots))
            same = jnp.where(first, d * scale, jnp.where(second, a * scale, same))
            beside = jnp.where(first | second, -(b * scale), beside)
        out[at : at + 8] = jnp.where(lane < at + 8, reduced * lax.rsqrt(pivots), 0.0)
        if p + 1 == panels:
            break
        partner = jnp.where(
            row % 2 == 0,
            jnp.concatenate([solved[1:], solved[:1]], axis=0),
            jnp.concatenate([solved[7:], solved[:7]], axis=0),
        )
        solved = same * solved + beside * partner
        pieces = [wide(solved[j : j + 1]) for j in range(8)]
        for q in range(p + 1, panels):
            terms = [wide(left[q][:, at + j : at + j + 1]) * pieces[j] for j in range(8)]
            left[q] = jnp.where(here, 0.0, left[q]) - tree_sum(terms)


def inverse_factor(gram):
    return pl.pallas_call(
        inverse_kernel,
        out_shape=jax.ShapeDtypeStruct((RANK, RANK), f32),
        compiler_params=pltpu.CompilerParams(vmem_limit_bytes=16 * MIB),
        cost_estimate=pl.CostEstimate(flops=3 * 10**9, bytes_accessed=10**5, transcendentals=0),
        name="inverse_factor",
    )(gram)


def factor_kernel(*refs):
    *parts, inverse, out = refs
    total = tree_sum([part[...] for part in parts])
    rows = dot_wide(total, inverse[...].T) * (1.0 / (32 * math.sqrt(FEATURES)))
    for i in range(out.shape[0]):
        out[i] = rows


def factor_rows(parts, inverse, copies):
    return pl.pallas_call(
        factor_kernel,
        out_shape=jax.ShapeDtypeStruct((copies,) + parts[0].shape, f32),
        compiler_params=pltpu.CompilerParams(vmem_limit_bytes=16 * MIB),
        cost_estimate=pl.CostEstimate(flops=10**8, bytes_accessed=4 * 10**5, transcendentals=0),
        name="factor_rows",
    )(*parts, inverse)


def join_kernel(right, inverse, out):
    out[:WIDTH] = right[...]
    out[WIDTH:] = inverse[...]


def join(right, inverse):
    return pl.pallas_call(
        join_kernel,
        out_shape=jax.ShapeDtypeStruct((WIDTH + RANK, RANK), f32),
        compiler_params=pltpu.CompilerParams(vmem_limit_bytes=8 * MIB),
        name="join",
    )(right, inverse)


def finish_kernel(which, merged, left_mean, joined, *rest):
    renewed, basis, factor, renewed_out, basis_out, turned, sems = rest[-7:]
    w = which[0]
    steps, rows, _ = renewed_out.shape

    def store(i):
        return pltpu.make_async_copy(renewed_out.at[i], renewed.at[w, pl.ds(i * rows, rows)], sems.at[i])

    store_factor = pltpu.make_async_copy(joined.at[pl.ds(0, WIDTH)], factor.at[w], sems.at[steps])
    store_basis = pltpu.make_async_copy(basis_out, basis.at[w], sems.at[steps + 1])
    store_factor.start()
    left_basis = dot_wide(left_mean[:, w].reshape(ROWS, RANK), joined[WIDTH:].T)
    basis_out[...] = left_basis
    store_basis.start()
    operand = stacked(left_basis * (1.0 / math.sqrt(FEATURES)))
    high, low = halves(joined[:WIDTH])
    turned[:, :RANK] = high
    turned[:, RANK : 2 * RANK] = high
    turned[:, 2 * RANK :] = low
    for i in range(steps):
        at = slice(i * rows, (i + 1) * rows)
        both = operand[at]
        approx = dot(both, turned[:, : 2 * RANK], NT) + dot(both[:, :RANK], turned[:, 2 * RANK :], NT)
        renewed_out[i] = merged[w, at] - approx
        store(i).start()
    store_factor.wait()
    store_basis.wait()
    for i in range(steps):
        store(i).wait()


def finish(which, merged, left_mean, joined, before=(), steps=2):
    rows = ROWS // steps
    return pl.pallas_call(
        finish_kernel,
        in_specs=[pl.BlockSpec(memory_space=pltpu.SMEM)]
        + [pl.BlockSpec(memory_space=pltpu.VMEM)] * 3
        + [pl.BlockSpec(memory_space=pl.ANY)] * len(before),
        out_specs=[pl.BlockSpec(memory_space=pl.ANY)] * 3,
        out_shape=[
            jax.ShapeDtypeStruct((MATRICES, ROWS, WIDTH), f32),
            jax.ShapeDtypeStruct((MATRICES, ROWS, RANK), f32),
            jax.ShapeDtypeStruct((MATRICES, WIDTH, RANK), f32),
        ],
        scratch_shapes=[
            pltpu.VMEM((steps, rows, WIDTH), f32),
            pltpu.VMEM((ROWS, RANK), f32),
            pltpu.VMEM((WIDTH, 3 * RANK), bf16),
            pltpu.SemaphoreType.DMA((steps + 2,)),
        ],
        input_output_aliases={4: 0, 5: 1, 6: 2} if before else {},
        compiler_params=pltpu.CompilerParams(vmem_limit_bytes=24 * MIB),
        cost_estimate=pl.CostEstimate(flops=8 * 10**8, bytes_accessed=6 * 10**6, transcendentals=0),
        name="finish",
    )(which, merged, left_mean, joined, *before)


def share_kernel(*refs, scale, count):
    parts, out = refs[:count], refs[-1]
    if count == 1:
        parts = [parts[0][i] for i in range(parts[0].shape[0])]
    else:
        parts = [part[0] for part in parts]
    total = tree_sum(parts) * scale
    for i in range(out.shape[0]):
        out[i] = total


def share(parts, copies, scale, after=()):
    parts = parts if isinstance(parts, list) else [parts]
    return pl.pallas_call(
        functools.partial(share_kernel, scale=scale, count=len(parts)),
        out_shape=jax.ShapeDtypeStruct((copies,) + parts[0].shape[1:], f32),
        compiler_params=pltpu.CompilerParams(vmem_limit_bytes=8 * MIB),
        name="share",
    )(*parts, *after)


def parcel_kernel(place, right, gram, arrived, out, gram_sum):
    gram_sum[...] = gram[...] + arrived[WIDTH:]
    piece = gram_sum[pl.ds(pl.multiple_of(place[0] * PIECE, PIECE), PIECE)]
    for i in range(BOX):
        at = slice(i * SHARE, (i + 1) * SHARE)
        out[i, :SHARE] = right[at] + arrived[at]
        out[i, SHARE:] = piece


def parcels(place, right, gram, arrived):
    return pl.pallas_call(
        parcel_kernel,
        in_specs=[pl.BlockSpec(memory_space=pltpu.SMEM)] + [pl.BlockSpec(memory_space=pltpu.VMEM)] * 3,
        out_shape=jax.ShapeDtypeStruct((BOX, SHARE + PIECE, RANK), f32),
        scratch_shapes=[pltpu.VMEM((RANK, RANK), f32)],
        compiler_params=pltpu.CompilerParams(vmem_limit_bytes=8 * MIB),
        name="parcels",
    )(place, right, gram, arrived)


def unpack_kernel(parts, total, gram):
    total[...] = tree_sum([parts[i, :SHARE] for i in range(BOX)])
    for k in range(RANK // PIECE):
        gram[k * PIECE : (k + 1) * PIECE] = tree_sum([parts[8 * x + k, SHARE:] for x in range(4)])


def unpack(parts):
    return pl.pallas_call(
        unpack_kernel,
        out_shape=[jax.ShapeDtypeStruct((SHARE, RANK), f32), jax.ShapeDtypeStruct((RANK, RANK), f32)],
        compiler_params=pltpu.CompilerParams(vmem_limit_bytes=8 * MIB),
        name="unpack",
    )(parts)


def exchange(x, axes):
    return lax.all_to_all(x, axes, 0, 0, tiled=True)


def swap(x):
    return lax.ppermute(x, "core", [(0, 1), (1, 0)])


def rounds(x, axis):
    return [x] + [lax.ppermute(x, axis, [(i, i ^ s) for i in range(4)]) for s in (1, 3, 2)]


def shards(gradient, feedback, right_prior):
    own = lax.axis_index("core")[None]
    other = 1 - own
    place = lax.axis_index(('zl', 'y'))[None]
    column, box = ('zl', 'y'), ('x', 'zl', 'y')
    gradient, feedback, right_prior = in_hbm(gradient[0]), in_hbm(feedback[0]), in_hbm(right_prior)
    left, merged = left_terms(other, place, gradient, feedback, right_prior)
    left = rounds(share(exchange(left, column), 1, 1.0 / 32), "zh")
    left_mean = exchange(share(left, 8, 1.0), column)

    right_other, gram = right_terms(other, merged, left_mean, True)
    arrived = swap(right_other)
    right = right_terms(own, merged, left_mean, False)[0]
    parts = exchange(parcels(place, right, gram, arrived), box)
    total, gram = unpack(parts)
    totals = rounds(total, "zh")
    inverse = inverse_factor(gram)
    right = exchange(factor_rows(totals, inverse, 32), box).reshape(WIDTH, RANK)
    joined = join(right, inverse)
    done = finish(own, merged, left_mean, joined)
    renewed, basis, factor = finish(other, merged, left_mean, swap(joined), tuple(done))
    return renewed[None], basis, factor


def solution(mesh):
    chips = Mesh(mesh.devices.reshape(4, 2, 4, 4, 2), ("zh", "zl", "y", "x", "core"))
    rep, fsdp = ("zh", "zl", "y"), ("x", "core")
    in_specs = (P(rep, None, fsdp, None), P(rep, None, fsdp, None), P())
    out_specs = (P(rep, None, fsdp, None), P(None, fsdp, None), P())
    return jax.shard_map(shards, mesh=chips, in_specs=in_specs, out_specs=out_specs, check_vma=False)
```
